32 devices in a mesh: row: 4 (over z), col: 8 (over y, x, core).
Axes of the slice: x: 2, y: 2, z: 4, core: 2. Of those that a mesh axis runs over, the one named last changes fastest.
Arguments:
- inputs: bfloat16 [512, 8192], P('row', 'col'), may hold values from -6 to 6
- grad_out: bfloat16 [512, 8192], P('row', 'col'), may hold values from -0.1796875 to 0.1796875
- gate_pre: bfloat16 [512, 28672], P('col', 'row'), may hold values from -6 to 6
- up_pre: bfloat16 [512, 28672], P('col', 'row'), may hold values from -6 to 6
- w_gate: bfloat16 [8192, 28672], P('col', 'row'), may hold values from -0.25 to 0.25
- w_up: bfloat16 [8192, 28672], P('col', 'row'), may hold values from -0.25 to 0.25
- w_down: bfloat16 [28672, 8192], P('row', 'col'), may hold values from -0.03125 to 0.03125
Outputs:
- grad_inputs: bfloat16 [512, 8192], P('row', 'col')
- grad_gate: bfloat16 [8192, 28672], P('col', 'row')
- grad_up: bfloat16 [8192, 28672], P('col', 'row')
- grad_down: bfloat16 [28672, 8192], P('row', 'col')
The draws below stay inside these ranges and needn't reach their ends.
All inputs are finite; a program needn't handle non-finite values.
Results may differ from the reference program's by a relative error of at most 0.005.
Values may be sent and summed in bfloat16 or wider, within the bound.
No kernel may reach another device: no remote copies, remote signals or barrier semaphores. Data moves between devices by JAX's collectives and lax.ppermute only.
A program may use at most 192 MiB of HBM per device.

```python
import jax
import jax.numpy as jnp
from jax import lax

D = 8192
FF = 28672
TOKENS = 512


def level_of(rng, dims, shards, low, top_value):
    loudness, own = 1.0, jax.random.fold_in(rng, 6)
    for axis_at, parts in shards:
        heights = jnp.exp(jax.random.uniform(jax.random.fold_in(own, axis_at), (parts,), jnp.float32, low / len(shards), top_value / len(shards)))
        loudness = loudness * jnp.repeat(heights, dims[axis_at] // parts).reshape([-1 if axis == axis_at else 1 for axis in range(len(dims))])
    return loudness


def noise(rng, shape, scale, reach, split=(), held_as=jnp.bfloat16):
    gain = level_of(rng, shape, split, -0.22, 0.18) if split else 1.0
    array = jax.random.normal(rng, shape, jnp.float32) * scale * gain
    return jnp.minimum(jnp.maximum(array, -reach), reach).astype(held_as)


def setup_inputs(seed: int = 0) -> dict:
    streams_of = jax.random.split(jax.random.key(seed), 8)
    return {
        "inputs": noise(streams_of[0], (TOKENS, D), 1.0, 6.0, ((0, 4), (1, 8))),
        "grad_out": noise(streams_of[1], (TOKENS, D), 0.03, 0.1796875, ((0, 4), (1, 8))),
        "gate_pre": noise(streams_of[2], (TOKENS, FF), 1.0, 6.0, ((0, 8), (1, 4))),
        "up_pre": noise(streams_of[3], (TOKENS, FF), 1.0, 6.0, ((0, 8), (1, 4))),
        "w_gate": noise(streams_of[4], (D, FF), (D // 16) ** -0.5, 0.25, ((0, 8), (1, 4))),
        "w_up": noise(streams_of[5], (D, FF), (D // 16) ** -0.5, 0.25, ((0, 8), (1, 4))),
        "w_down": noise(streams_of[6], (FF, D), FF ** -0.5, 0.03125, ((0, 4), (1, 8))),
    }


def swiglu_back(gate_pre, up_pre, hidden_grad):
    gate_wide = gate_pre.astype(jnp.float32)
    up_wide = up_pre.astype(jnp.float32)
    logistic = jax.nn.sigmoid(gate_wide)
    swished = gate_wide * logistic
    hidden = (swished * up_wide).astype(jnp.bfloat16)
    up_grad = (hidden_grad * swished).astype(jnp.bfloat16)
    gate_grad = (hidden_grad * up_wide * logistic * (1.0 + gate_wide * (1.0 - logistic))).astype(jnp.bfloat16)
    return hidden, gate_grad, up_grad


def reference(inputs, grad_out, gate_pre, up_pre, w_gate, w_up, w_down):
    last_last = (((1,), (1,)), ((), ()))
    first_first = (((0,), (0,)), ((), ()))
    hidden_grad = lax.dot_general(grad_out, w_down, last_last, preferred_element_type=jnp.float32)
    hidden, gate_grad, up_grad = swiglu_back(gate_pre, up_pre, hidden_grad)
    grad_down = lax.dot_general(hidden, grad_out, first_first, preferred_element_type=jnp.float32).astype(jnp.bfloat16)
    grad_gate = lax.dot_general(inputs, gate_grad, first_first, preferred_element_type=jnp.float32).astype(jnp.bfloat16)
    grad_up = lax.dot_general(inputs, up_grad, first_first, preferred_element_type=jnp.float32).astype(jnp.bfloat16)
    grad_inputs = lax.dot_general(gate_grad, w_gate, last_last, preferred_element_type=jnp.float32)
    grad_inputs = grad_inputs + lax.dot_general(up_grad, w_up, last_last, preferred_element_type=jnp.float32)
    return grad_inputs.astype(jnp.bfloat16), grad_gate, grad_up, grad_down
```

```python
import functools

import jax
import jax.numpy as jnp
from jax import lax
from jax.experimental import pallas as pl
from jax.experimental.pallas import tpu as pltpu
from jax.sharding import PartitionSpec as P

BF16, F32 = jnp.bfloat16, jnp.float32
VMEM_BYTES = 56 * 1024 * 1024


def dot(a, b, a_dim, b_dim):
    return lax.dot_general(a, b, (((a_dim,), (b_dim,)), ((), ())), preferred_element_type=F32)


def logistic_of(wide):
    return 0.5 + 0.5 * jnp.tanh(0.5 * wide)


def swiglu_back(gate_pre, up_pre, hidden_grad):
    gate_wide = gate_pre.astype(F32)
    up_wide = up_pre.astype(F32)
    logistic = logistic_of(gate_wide)
    swished = gate_wide * logistic
    up_grad = (hidden_grad * swished).astype(BF16)
    gate_grad = (hidden_grad * up_wide * logistic * (1.0 + gate_wide * (1.0 - logistic))).astype(BF16)
    return gate_grad, up_grad


def hidden_of(gate_pre, up_pre):
    gate_wide = gate_pre.astype(F32)
    return (gate_wide * logistic_of(gate_wide) * up_pre.astype(F32)).astype(BF16)


def params():
    return pltpu.CompilerParams(vmem_limit_bytes=VMEM_BYTES)


def after(array, before):
    return lax.optimization_barrier((array, before))[0]


def whole_block(shape):
    return pl.BlockSpec(shape, lambda *_: (0,) * len(shape))


def swap(array, bit):
    return lax.ppermute(array, "col", [(i, i ^ bit) for i in range(8)])


def onward(array, rows, step):
    return lax.ppermute(array, "row", [(i, (i + step) % rows) for i in range(rows)])


def token_block(place, col):
    return (((place << 1) & 7) | (place >> 2)) ^ col


def place_of(block, col):
    offset = block ^ col
    return (offset >> 1) + 4 * (offset & 1)


def arrange(where, blocks):
    rows, (count, features) = len(blocks), blocks[0].shape
    tokens = rows * count
    part = tokens // 8

    def kernel(where_ref, *refs):
        *ins, out = refs
        row, col = where_ref[0], where_ref[1]
        for step, ref in enumerate(ins):
            owner = lax.rem(row + (rows - step), rows)
            for at in range(8 // rows):
                start = pl.multiple_of(place_of(owner * (8 // rows) + at, col) * part, part)
                out[pl.ds(start, part), :] = ref[at * part : (at + 1) * part, :]

    return pl.pallas_call(
        kernel,
        out_shape=jax.ShapeDtypeStruct((tokens, features), BF16),
        in_specs=[pl.BlockSpec(memory_space=pltpu.SMEM)] + [pl.BlockSpec(memory_space=pltpu.VMEM)] * rows,
        out_specs=pl.BlockSpec(memory_space=pltpu.VMEM),
        compiler_params=params(),
        name="arrange",
    )(where, *blocks)


def reorder(where, natural):
    tokens, features = natural.shape
    part = tokens // 8

    def kernel(where_ref, x, out):
        for place in range(8):
            start = pl.multiple_of(token_block(place, where_ref[1]) * part, part)
            out[place * part : (place + 1) * part, :] = x[pl.ds(start, part), :]

    return pl.pallas_call(
        kernel,
        out_shape=jax.ShapeDtypeStruct((tokens, features), BF16),
        in_specs=[pl.BlockSpec(memory_space=pltpu.SMEM), pl.BlockSpec(memory_space=pltpu.VMEM)],
        out_specs=pl.BlockSpec(memory_space=pltpu.VMEM),
        compiler_params=params(),
        name="reorder",
    )(where, natural)


def sum_rows(blocks):
    def kernel(own, *refs):
        *ins, out = refs
        total = own[...]
        for ref in ins:
            total = total + ref[...].astype(F32)
        out[...] = total.astype(BF16)

    return pl.pallas_call(
        kernel,
        out_shape=jax.ShapeDtypeStruct(blocks[0].shape, BF16),
        compiler_params=params(),
        name="sum_rows",
    )(*blocks)


def partial_hidden_grad(here, there, w_here, w_there, start, size, tile):
    tokens, features = here.shape
    part = tokens // 4

    def kernel(x, y, w, v, own, for_x, for_y, for_far):
        product = dot(x[...], w[...], 1, 1) + dot(y[...], v[...], 1, 1)
        own[...] = product[:part]
        for_x[...] = product[part : 2 * part].astype(BF16)
        for_y[...] = product[2 * part : 3 * part].astype(BF16)
        for_far[...] = product[3 * part :].astype(BF16)

    column = pl.BlockSpec((part, tile), lambda i: (0, i))
    weights = pl.BlockSpec((tile, features), lambda i: (i + start // tile, 0))
    sent = jax.ShapeDtypeStruct((part, size), BF16)
    return pl.pallas_call(
        kernel,
        grid=(size // tile,),
        in_specs=[whole_block((tokens, features))] * 2 + [weights] * 2,
        out_specs=[column] * 4,
        out_shape=[jax.ShapeDtypeStruct((part, size), F32), sent, sent, sent],
        compiler_params=params(),
        name="partial_hidden_grad",
    )(here, there, w_here, w_there)


def total_hidden_grad(own, *received):
    def kernel(a, b, c, d, out):
        out[...] = (a[...] + b[...].astype(F32) + c[...].astype(F32) + d[...].astype(F32)).astype(BF16)

    return pl.pallas_call(
        kernel,
        out_shape=jax.ShapeDtypeStruct(own.shape, BF16),
        compiler_params=params(),
        name="total_hidden_grad",
    )(own, *received)


def spread_whole(block, over_x_first):
    at_x, at_y = swap(block, 2), swap(block, 4)
    return block, at_x, at_y, swap(at_x, 4) if over_x_first else swap(at_y, 2)


def unpack(block):
    part = block.shape[0] // 8
    gate = jnp.concatenate([block[2 * i * part : (2 * i + 1) * part] for i in range(4)], axis=0)
    up = jnp.concatenate([block[(2 * i + 1) * part : (2 * i + 2) * part] for i in range(4)], axis=0)
    return gate, up


def grad_down_part(stored, grad_out_all, grad_down, hidden_units, inside, start, size, tile):
    tokens, features = grad_out_all.shape

    def kernel(p0, p1, x, *rest):
        out = rest[-1]
        hidden = jnp.concatenate([hidden_of(*unpack(p0[...])), hidden_of(*unpack(p1[...]))], axis=0)
        out[...] = dot(hidden, x[...], 0, 0).astype(BF16)

    block = pl.BlockSpec((tokens, tile), lambda i: (0, i + inside // tile))
    earlier = [] if grad_down is None else [grad_down]
    return pl.pallas_call(
        kernel,
        grid=(size // tile,),
        in_specs=[block] * 2
        + [whole_block((tokens, features))]
        + [pl.BlockSpec(memory_space=pl.ANY)] * len(earlier),
        out_specs=pl.BlockSpec((tile, features), lambda i: (i + start // tile, 0)),
        out_shape=jax.ShapeDtypeStruct((hidden_units, features), BF16),
        input_output_aliases={3: 0} if earlier else {},
        compiler_params=params(),
        name="grad_down_part",
    )(*stored, grad_out_all, *earlier)


def both_gradients(where, hidden_grad, p0, p1):
    part = hidden_grad.shape[0] // 8
    rows = []
    for place in range(8):
        start = pl.multiple_of(token_block(place, where[1]) * part, part)
        rows.append(hidden_grad[pl.ds(start, part), :])
    a0, b0 = swiglu_back(*unpack(p0[...]), jnp.concatenate(rows[:4], axis=0).astype(F32))
    a1, b1 = swiglu_back(*unpack(p1[...]), jnp.concatenate(rows[4:], axis=0).astype(F32))
    return jnp.concatenate([a0, a1], axis=0), jnp.concatenate([b0, b1], axis=0)


def first_part(where, hidden_grad, stored, inputs_all, w_gate, w_up, size, tile):
    tokens, features = inputs_all.shape

    def kernel(where_ref, h, p0, p1, x, wg, wu, grad_gate, grad_up, total):
        gate_grad, up_grad = both_gradients(where_ref, h, p0, p1)
        grad_gate[...] = dot(x[...], gate_grad, 0, 0).astype(BF16)
        grad_up[...] = dot(x[...], up_grad, 0, 0).astype(BF16)
        more = dot(gate_grad, wg[...], 1, 1) + dot(up_grad, wu[...], 1, 1)

        @pl.when(pl.program_id(0) == 0)
        def _():
            total[...] = more

        @pl.when(pl.program_id(0) > 0)
        def _():
            total[...] += more

    block = pl.BlockSpec((tokens, tile), lambda i: (0, i))
    column = pl.BlockSpec((features, tile), lambda i: (0, i))
    weights = jax.ShapeDtypeStruct(w_gate.shape, BF16)
    return pl.pallas_call(
        kernel,
        grid=(size // tile,),
        in_specs=[pl.BlockSpec(memory_space=pltpu.SMEM)]
        + [block] * 3
        + [whole_block((tokens, features)), column, column],
        out_specs=[column, column, whole_block((tokens, features))],
        out_shape=[weights, weights, jax.ShapeDtypeStruct((tokens, features), F32)],
        compiler_params=params(),
        name="first_part",
    )(where, hidden_grad, *stored, inputs_all, w_gate, w_up)


def input_part(where, rows, hidden_grad, stored, w_gate, w_up, total, start, size, tile):
    tokens, features = total.shape
    part = tokens // 8
    steps = size // tile
    strip = features // steps

    def kernel(where_ref, h, p0, p1, wg, wu, before, gate_out, up_out, *rest):
        *outs, carry = rest
        gate_grad, up_grad = both_gradients(where_ref, h, p0, p1)
        gate_out[...] = gate_grad
        up_out[...] = up_grad
        more = dot(gate_grad, wg[...], 1, 1) + dot(up_grad, wu[...], 1, 1)
        step = pl.program_id(0)

        @pl.when(step == 0)
        def _():
            carry[...] = more

        @pl.when(step > 0)
        def _():
            carry[...] += more

        carry[:, pl.ds(pl.multiple_of(step * strip, strip), strip)] += before[...]

        @pl.when(step == steps - 1)
        def _():
            row, col = where_ref[0], where_ref[1]
            for ahead, out in enumerate(outs):
                owner = lax.rem(row + ahead, rows)
                for at in range(8 // rows):
                    place = pl.multiple_of(place_of(owner * (8 // rows) + at, col) * part, part)
                    out[at * part : (at + 1) * part, :] = carry[pl.ds(place, part), :].astype(out.dtype)

    block = pl.BlockSpec((tokens, tile), lambda i: (0, i))
    column = pl.BlockSpec((features, tile), lambda i: (0, i + start // tile))
    made = jax.ShapeDtypeStruct((tokens, size), BF16)
    shape = (tokens // rows, features)
    return pl.pallas_call(
        kernel,
        grid=(steps,),
        in_specs=[pl.BlockSpec(memory_space=pltpu.SMEM)]
        + [block] * 3
        + [column, column, pl.BlockSpec((tokens, strip), lambda i: (0, i))],
        out_specs=[block, block] + [whole_block(shape)] * rows,
        out_shape=[made, made]
        + [jax.ShapeDtypeStruct(shape, F32)]
        + [jax.ShapeDtypeStruct(shape, BF16)] * (rows - 1),
        scratch_shapes=[pltpu.VMEM((tokens, features), F32)],
        compiler_params=params(),
        name="input_part",
    )(where, hidden_grad, *stored, w_gate, w_up, total)


def weight_part(gate_grad, up_grad, inputs_all, grad_gate, grad_up, start, tile):
    tokens, features = inputs_all.shape
    size = gate_grad.shape[1]

    def kernel(a, b, x, _, __, gate_out, up_out):
        gate_out[...] = dot(x[...], a[...], 0, 0).astype(BF16)
        up_out[...] = dot(x[...], b[...], 0, 0).astype(BF16)

    block = pl.BlockSpec((tokens, tile), lambda i: (0, i))
    column = pl.BlockSpec((features, tile), lambda i: (0, i + start // tile))
    weights = jax.ShapeDtypeStruct(grad_gate.shape, BF16)
    return pl.pallas_call(
        kernel,
        grid=(size // tile,),
        in_specs=[block, block, whole_block((tokens, features))] + [pl.BlockSpec(memory_space=pl.ANY)] * 2,
        out_specs=[column, column],
        out_shape=[weights, weights],
        input_output_aliases={3: 0, 4: 1},
        compiler_params=params(),
        name="weight_part",
    )(gate_grad, up_grad, inputs_all, grad_gate, grad_up)


def pack(pieces):
    size = pieces[0].shape[1]
    tile = size // 2
    rows = [piece.shape[0] for piece in pieces]

    def kernel(*refs):
        *ins, out = refs
        start = 0
        for ref, count in zip(ins, rows):
            out[start : start + count, :] = ref[...]
            start += count

    return pl.pallas_call(
        kernel,
        grid=(2,),
        in_specs=[pl.BlockSpec((count, tile), lambda i: (0, i)) for count in rows],
        out_specs=pl.BlockSpec((sum(rows), tile), lambda i: (0, i)),
        out_shape=jax.ShapeDtypeStruct((sum(rows), size), BF16),
        compiler_params=params(),
        name="pack",
    )(*pieces)


def both_cores(pieces):
    mine = pack(pieces)
    return mine, swap(mine, 1)


def on_square(rows, inputs, grad_out, gate_pre, up_pre, w_gate, w_up, w_down):
    hidden_units = w_gate.shape[1]
    unit = 1024
    cut = 3 * unit
    chunks = ((0, cut), (cut, hidden_units - cut))
    part = gate_pre.shape[0]
    tokens = 8 * part
    where = jnp.stack([lax.axis_index("row"), lax.axis_index("col")]).astype(jnp.int32)

    def stack(at):
        start, size = chunks[at]
        return jnp.concatenate([gate_pre[:, start : start + size], up_pre[:, start : start + size]], axis=0)

    def hidden_part(at, before):
        start, size = chunks[at]
        own, *sent = partial_hidden_grad(after(here, before), grad_out_there, w_down, w_there, start, size, unit)
        return own, sent

    def send_hidden(sent):
        return [swap(block, bits) for block, bits in zip(sent, (2, 4, 6))]

    def down(at, grad_down, before):
        start, size = chunks[at]
        return grad_down_part(
            stored[at], after(grad_out_all, before), grad_down, hidden_units, 0, start, size, unit
        )

    stored = {}
    grad_out_all = arrange(where, [grad_out] + [onward(grad_out, rows, step) for step in range(1, rows)])
    w_there = swap(w_down, 1)
    both0, both1 = stack(0), stack(1)
    x0, y0 = swap(both0, 2), swap(both0, 4)
    far0 = [swap(x0[:part], 4), swap(y0[part:], 2)]
    x1, y1 = swap(both1, 2), swap(both1, 4)
    here = grad_out_all[: tokens // 2]
    grad_out_there = swap(grad_out_all[tokens // 2 :], 1)
    inputs_all = lax.all_gather(after(inputs, here), "row", axis=0, tiled=True)

    own0, sent0 = hidden_part(0, here)
    got0 = send_hidden(sent0)
    own1, sent1 = hidden_part(1, own0)
    x0, y0, *far0 = [after(piece, own1) for piece in (x0, y0, *far0)]
    stored[0] = both_cores([both0, x0, y0, *far0])
    x1, y1 = after(x1, stored[0][0]), after(y1, stored[0][0])
    far1 = [swap(x1[:part], 4), swap(y1[part:], 2)]
    hidden0 = total_hidden_grad(after(own0, (x1, y1)), *got0)
    hidden0_all = lax.all_gather(hidden0, "col", axis=0, tiled=True)
    got1 = send_hidden(sent1)
    inputs_all = reorder(where, after(inputs_all, hidden0))
    grad_down = down(0, None, inputs_all)
    hidden1 = total_hidden_grad(after(own1, grad_down), *got1)
    hidden1_all = lax.all_gather(hidden1, "col", axis=0, tiled=True)
    stored[1] = both_cores([after(piece, hidden1) for piece in (both1, x1, y1, *far1)])
    grad_gate, grad_up, total = first_part(
        where, hidden0_all, stored[0], after(inputs_all, stored[1][0]), w_gate, w_up, cut, unit // 2
    )
    gate_grad, up_grad, *sums = input_part(
        where, rows, hidden1_all, stored[1], w_gate, w_up, total, *chunks[1], unit // 2
    )
    sums = [sums[0]] + [onward(block, rows, ahead) for ahead, block in enumerate(sums) if ahead]
    grad_gate, grad_up = weight_part(gate_grad, up_grad, inputs_all, grad_gate, grad_up, cut, unit // 2)
    grad_down = down(1, grad_down, grad_up)
    grad_inputs = sum_rows([after(sums[0], grad_down)] + sums[1:])
    return grad_inputs, grad_gate, grad_up, grad_down


def on_any(inputs, grad_out, gate_pre, up_pre, w_gate, w_up, w_down):
    inputs_all = lax.all_gather(inputs, "row", axis=0, tiled=True)
    grad_out_all = lax.all_gather(grad_out, "row", axis=0, tiled=True)
    gate_all = lax.all_gather(gate_pre, "col", axis=0, tiled=True)
    up_all = lax.all_gather(up_pre, "col", axis=0, tiled=True)
    hidden_grad = lax.psum_scatter(dot(grad_out_all, w_down, 1, 1), "col", scatter_dimension=0, tiled=True)
    gate_grad, up_grad = swiglu_back(gate_pre, up_pre, hidden_grad)
    gate_grad = lax.all_gather(gate_grad, "col", axis=0, tiled=True)
    up_grad = lax.all_gather(up_grad, "col", axis=0, tiled=True)
    grad_down = dot(hidden_of(gate_all, up_all), grad_out_all, 0, 0).astype(BF16)
    grad_gate = dot(inputs_all, gate_grad, 0, 0).astype(BF16)
    grad_up = dot(inputs_all, up_grad, 0, 0).astype(BF16)
    total = dot(gate_grad, w_gate, 1, 1) + dot(up_grad, w_up, 1, 1)
    grad_inputs = lax.psum_scatter(total, "row", scatter_dimension=0, tiled=True).astype(BF16)
    return grad_inputs, grad_gate, grad_up, grad_down


def solution(mesh):
    rows, cols = mesh.shape["row"], mesh.shape["col"]
    plan = functools.partial(on_square, rows) if (rows, cols) == (4, 8) else on_any
    placed = (
        P("row", "col"),
        P("row", "col"),
        P("col", "row"),
        P("col", "row"),
        P("col", "row"),
        P("col", "row"),
        P("row", "col"),
    )
    return jax.shard_map(
        plan,
        mesh=mesh,
        in_specs=placed,
        out_specs=(P("row", "col"), P("col", "row"), P("col", "row"), P("row", "col")),
        check_vma=False,
    )
```

```python
import functools

import jax
import jax.numpy as jnp
from jax import lax
from jax.experimental import pallas as pl
from jax.experimental.pallas import tpu as pltpu
from jax.sharding import PartitionSpec as P

BF16, F32 = jnp.bfloat16, jnp.float32
VMEM_BYTES = 56 * 1024 * 1024


def dot(a, b, a_dim, b_dim):
    return lax.dot_general(a, b, (((a_dim,), (b_dim,)), ((), ())), preferred_element_type=F32)


def logistic_of(wide):
    return 0.5 + 0.5 * jnp.tanh(0.5 * wide)


def swiglu_back(gate_pre, up_pre, hidden_grad):
    gate_wide = gate_pre.astype(F32)
    up_wide = up_pre.astype(F32)
    logistic = logistic_of(gate_wide)
    swished = gate_wide * logistic
    up_grad = (hidden_grad * swished).astype(BF16)
    gate_grad = (hidden_grad * up_wide * logistic * (1.0 + gate_wide * (1.0 - logistic))).astype(BF16)
    return gate_grad, up_grad


def hidden_of(gate_pre, up_pre):
    gate_wide = gate_pre.astype(F32)
    return (gate_wide * logistic_of(gate_wide) * up_pre.astype(F32)).astype(BF16)


def params():
    return pltpu.CompilerParams(vmem_limit_bytes=VMEM_BYTES)


def after(array, before):
    return lax.optimization_barrier((array, before))[0]


def whole_block(shape):
    return pl.BlockSpec(shape, lambda *_: (0,) * len(shape))


def swap(array, bit):
    return lax.ppermute(array, "col", [(i, i ^ bit) for i in range(8)])


def onward(array, rows, step):
    return lax.ppermute(array, "row", [(i, (i + step) % rows) for i in range(rows)])


def token_block(place, col):
    return (((place << 1) & 7) | (place >> 2)) ^ col


def place_of(block, col):
    offset = block ^ col
    return (offset >> 1) + 4 * (offset & 1)


def reorder(where, natural):
    tokens, features = natural.shape
    part = tokens // 8

    def kernel(where_ref, x, out, second):
        for place in range(8):
            start = pl.multiple_of(token_block(place, where_ref[1]) * part, part)
            rows = x[pl.ds(start, part), :]
            out[place * part : (place + 1) * part, :] = rows
            if place >= 4:
                second[(place - 4) * part : (place - 3) * part, :] = rows

    return pl.pallas_call(
        kernel,
        out_shape=[
            jax.ShapeDtypeStruct((tokens, features), BF16),
            jax.ShapeDtypeStruct((tokens // 2, features), BF16),
        ],
        in_specs=[pl.BlockSpec(memory_space=pltpu.SMEM), pl.BlockSpec(memory_space=pltpu.VMEM)],
        out_specs=[pl.BlockSpec(memory_space=pltpu.VMEM)] * 2,
        compiler_params=params(),
        name="reorder",
    )(where, natural)


def sum_rows(blocks):
    def kernel(own, *refs):
        *ins, out = refs
        total = own[...]
        for ref in ins:
            total = total + ref[...].astype(F32)
        out[...] = total.astype(BF16)

    return pl.pallas_call(
        kernel,
        out_shape=jax.ShapeDtypeStruct(blocks[0].shape, BF16),
        compiler_params=params(),
        name="sum_rows",
    )(*blocks)


def partial_hidden_grad(here, there, w_here, w_there, start, size, tile):
    tokens, features = there.shape
    part = tokens // 4

    def kernel(x, y, w, v, own, for_x, for_y, for_far):
        product = dot(x[...], w[...], 1, 1) + dot(y[...], v[...], 1, 1)
        own[...] = product[:part]
        for_x[...] = product[part : 2 * part].astype(BF16)
        for_y[...] = product[2 * part : 3 * part].astype(BF16)
        for_far[...] = product[3 * part :].astype(BF16)

    column = pl.BlockSpec((part, tile), lambda i: (0, i))
    weights = pl.BlockSpec((tile, features), lambda i: (i + start // tile, 0))
    sent = jax.ShapeDtypeStruct((part, size), BF16)
    return pl.pallas_call(
        kernel,
        grid=(size // tile,),
        in_specs=[whole_block((tokens, features))] * 2 + [weights] * 2,
        out_specs=[column] * 4,
        out_shape=[jax.ShapeDtypeStruct((part, size), F32), sent, sent, sent],
        compiler_params=params(),
        name="partial_hidden_grad",
    )(here, there, w_here, w_there)


def total_hidden_grad(own, *received):
    def kernel(a, b, c, d, out):
        out[...] = (a[...] + b[...].astype(F32) + c[...].astype(F32) + d[...].astype(F32)).astype(BF16)

    return pl.pallas_call(
        kernel,
        out_shape=jax.ShapeDtypeStruct(own.shape, BF16),
        compiler_params=params(),
        name="total_hidden_grad",
    )(own, *received)


def spread_whole(block, over_x_first):
    at_x, at_y = swap(block, 2), swap(block, 4)
    return block, at_x, at_y, swap(at_x, 4) if over_x_first else swap(at_y, 2)


def unpack(block):
    part = block.shape[0] // 8
    gate = jnp.concatenate([block[2 * i * part : (2 * i + 1) * part] for i in range(4)], axis=0)
    up = jnp.concatenate([block[(2 * i + 1) * part : (2 * i + 2) * part] for i in range(4)], axis=0)
    return gate, up


def grad_down_part(stored, grad_out_all, grad_down, hidden_units, inside, start, size, tile):
    tokens, features = grad_out_all.shape

    def kernel(p0, p1, x, *rest):
        out = rest[-1]
        hidden = jnp.concatenate([hidden_of(*unpack(p0[...])), hidden_of(*unpack(p1[...]))], axis=0)
        out[...] = dot(hidden, x[...], 0, 0).astype(BF16)

    block = pl.BlockSpec((tokens, tile), lambda i: (0, i + inside // tile))
    earlier = [] if grad_down is None else [grad_down]
    return pl.pallas_call(
        kernel,
        grid=(size // tile,),
        in_specs=[block] * 2
        + [whole_block((tokens, features))]
        + [pl.BlockSpec(memory_space=pl.ANY)] * len(earlier),
        out_specs=pl.BlockSpec((tile, features), lambda i: (i + start // tile, 0)),
        out_shape=jax.ShapeDtypeStruct((hidden_units, features), BF16),
        input_output_aliases={3: 0} if earlier else {},
        compiler_params=params(),
        name="grad_down_part",
    )(*stored, grad_out_all, *earlier)


def both_gradients(where, hidden_grad, p0, p1):
    part = hidden_grad.shape[0] // 8
    rows = []
    for place in range(8):
        start = pl.multiple_of(token_block(place, where[1]) * part, part)
        rows.append(hidden_grad[pl.ds(start, part), :])
    a0, b0 = swiglu_back(*unpack(p0[...]), jnp.concatenate(rows[:4], axis=0).astype(F32))
    a1, b1 = swiglu_back(*unpack(p1[...]), jnp.concatenate(rows[4:], axis=0).astype(F32))
    return jnp.concatenate([a0, a1], axis=0), jnp.concatenate([b0, b1], axis=0)


def first_part(where, hidden_grad, stored, inputs_all, w_gate, w_up, size, tile):
    tokens, features = inputs_all.shape

    def kernel(where_ref, h, p0, p1, x, wg, wu, grad_gate, grad_up, total):
        gate_grad, up_grad = both_gradients(where_ref, h, p0, p1)
        grad_gate[...] = dot(x[...], gate_grad, 0, 0).astype(BF16)
        grad_up[...] = dot(x[...], up_grad, 0, 0).astype(BF16)
        more = dot(gate_grad, wg[...], 1, 1) + dot(up_grad, wu[...], 1, 1)

        @pl.when(pl.program_id(0) == 0)
        def _():
            total[...] = more

        @pl.when(pl.program_id(0) > 0)
        def _():
            total[...] += more

    block = pl.BlockSpec((tokens, tile), lambda i: (0, i))
    column = pl.BlockSpec((features, tile), lambda i: (0, i))
    weights = jax.ShapeDtypeStruct(w_gate.shape, BF16)
    return pl.pallas_call(
        kernel,
        grid=(size // tile,),
        in_specs=[pl.BlockSpec(memory_space=pltpu.SMEM)]
        + [block] * 3
        + [whole_block((tokens, features)), column, column],
        out_specs=[column, column, whole_block((tokens, features))],
        out_shape=[weights, weights, jax.ShapeDtypeStruct((tokens, features), F32)],
        compiler_params=params(),
        name="first_part",
    )(where, hidden_grad, *stored, inputs_all, w_gate, w_up)


def input_part(where, rows, hidden_grad, stored, w_gate, w_up, total, start, size, tile):
    tokens, features = total.shape
    part = tokens // 8
    steps = size // tile
    strip = features // steps

    def kernel(where_ref, h, p0, p1, wg, wu, before, gate_out, up_out, *rest):
        *outs, carry = rest
        gate_grad, up_grad = both_gradients(where_ref, h, p0, p1)
        gate_out[...] = gate_grad
        up_out[...] = up_grad
        more = dot(gate_grad, wg[...], 1, 1) + dot(up_grad, wu[...], 1, 1)
        step = pl.program_id(0)

        @pl.when(step == 0)
        def _():
            carry[...] = more

        @pl.when(step > 0)
        def _():
            carry[...] += more

        carry[:, pl.ds(pl.multiple_of(step * strip, strip), strip)] += before[...]

        @pl.when(step == steps - 1)
        def _():
            row, col = where_ref[0], where_ref[1]
            for ahead, out in enumerate(outs):
                owner = lax.rem(row + ahead, rows)
                for at in range(8 // rows):
                    place = pl.multiple_of(place_of(owner * (8 // rows) + at, col) * part, part)
                    out[at * part : (at + 1) * part, :] = carry[pl.ds(place, part), :].astype(out.dtype)

    block = pl.BlockSpec((tokens, tile), lambda i: (0, i))
    column = pl.BlockSpec((features, tile), lambda i: (0, i + start // tile))
    made = jax.ShapeDtypeStruct((tokens, size), BF16)
    shape = (tokens // rows, features)
    return pl.pallas_call(
        kernel,
        grid=(steps,),
        in_specs=[pl.BlockSpec(memory_space=pltpu.SMEM)]
        + [block] * 3
        + [column, column, pl.BlockSpec((tokens, strip), lambda i: (0, i))],
        out_specs=[block, block] + [whole_block(shape)] * rows,
        out_shape=[made, made]
        + [jax.ShapeDtypeStruct(shape, F32)]
        + [jax.ShapeDtypeStruct(shape, BF16)] * (rows - 1),
        scratch_shapes=[pltpu.VMEM((tokens, features), F32)],
        compiler_params=params(),
        name="input_part",
    )(where, hidden_grad, *stored, w_gate, w_up, total)


def weight_part(gate_grad, up_grad, inputs_all, grad_gate, grad_up, start, tile):
    tokens, features = inputs_all.shape
    size = gate_grad.shape[1]

    def kernel(a, b, x, _, __, gate_out, up_out):
        gate_out[...] = dot(x[...], a[...], 0, 0).astype(BF16)
        up_out[...] = dot(x[...], b[...], 0, 0).astype(BF16)

    block = pl.BlockSpec((tokens, tile), lambda i: (0, i))
    column = pl.BlockSpec((features, tile), lambda i: (0, i + start // tile))
    weights = jax.ShapeDtypeStruct(grad_gate.shape, BF16)
    return pl.pallas_call(
        kernel,
        grid=(size // tile,),
        in_specs=[block, block, whole_block((tokens, features))] + [pl.BlockSpec(memory_space=pl.ANY)] * 2,
        out_specs=[column, column],
        out_shape=[weights, weights],
        input_output_aliases={3: 0, 4: 1},
        compiler_params=params(),
        name="weight_part",
    )(gate_grad, up_grad, inputs_all, grad_gate, grad_up)


def pack(pieces):
    size = pieces[0].shape[1]
    tile = size // 2
    rows = [piece.shape[0] for piece in pieces]

    def kernel(*refs):
        *ins, out = refs
        start = 0
        for ref, count in zip(ins, rows):
            out[start : start + count, :] = ref[...]
            start += count

    return pl.pallas_call(
        kernel,
        grid=(2,),
        in_specs=[pl.BlockSpec((count, tile), lambda i: (0, i)) for count in rows],
        out_specs=pl.BlockSpec((sum(rows), tile), lambda i: (0, i)),
        out_shape=jax.ShapeDtypeStruct((sum(rows), size), BF16),
        compiler_params=params(),
        name="pack",
    )(*pieces)


def both_cores(pieces):
    mine = pack(pieces)
    return mine, swap(mine, 1)


def on_square(rows, inputs, grad_out, gate_pre, up_pre, w_gate, w_up, w_down):
    hidden_units = w_gate.shape[1]
    unit = 1024
    cut = 3 * unit
    chunks = ((0, cut), (cut, hidden_units - cut))
    part = gate_pre.shape[0]
    tokens = 8 * part
    where = jnp.stack([lax.axis_index("row"), lax.axis_index("col")]).astype(jnp.int32)

    def stack(at):
        start, size = chunks[at]
        return jnp.concatenate([gate_pre[:, start : start + size], up_pre[:, start : start + size]], axis=0)

    def hidden_part(at, before):
        start, size = chunks[at]
        own, *sent = partial_hidden_grad(after(here, before), grad_out_there, w_down, w_there, start, size, unit)
        return own, sent

    def send_hidden(sent):
        return [swap(block, bits) for block, bits in zip(sent, (2, 4, 6))]

    def down(at, grad_down, before):
        start, size = chunks[at]
        return grad_down_part(
            stored[at], after(grad_out_all, before), grad_down, hidden_units, 0, start, size, unit
        )

    stored = {}
    grad_out_all = lax.all_gather(grad_out, "row", axis=0, tiled=True)
    w_there = swap(w_down, 1)
    both0, both1 = stack(0), stack(1)
    x0, y0 = swap(both0, 2), swap(both0, 4)
    x0, y0 = after(x0, both1), after(y0, both1)
    over_y, over_x = x0[:part], y0[part:]
    far0 = [swap(over_y, 4), swap(over_x, 2)]
    both1 = after(both1, (over_y, over_x))
    x1, y1 = swap(both1, 2), swap(both1, 4)
    grad_out_all, for_peer = reorder(where, after(grad_out_all, (far0, w_there)))
    here = grad_out_all
    grad_out_there = swap(for_peer, 1)
    inputs_all = lax.all_gather(after(inputs, here), "row", axis=0, tiled=True)

    own0, sent0 = hidden_part(0, here)
    got0 = send_hidden(sent0)
    own1, sent1 = hidden_part(1, (own0, x1, y1))
    got1 = send_hidden(sent1)
    hidden0 = total_hidden_grad(after(own0, own1), *got0)
    hidden0_all = lax.all_gather(hidden0, "col", axis=0, tiled=True)
    stored[0] = both_cores([both0, x0, y0, *[after(piece, hidden0) for piece in far0]])
    x1, y1 = after(x1, stored[0][0]), after(y1, stored[0][0])
    over_y, over_x = x1[:part], y1[part:]
    grad_down = down(0, None, (over_y, over_x))
    far1 = [swap(over_y, 4), swap(over_x, 2)]
    inputs_all, _ = reorder(where, after(inputs_all, grad_down))
    hidden1 = total_hidden_grad(after(own1, inputs_all), *got1)
    hidden1_all = lax.all_gather(hidden1, "col", axis=0, tiled=True)
    grad_gate, grad_up, total = first_part(
        where, hidden0_all, stored[0], after(inputs_all, hidden1), w_gate, w_up, cut, unit // 2
    )
    stored[1] = both_cores([after(piece, total) for piece in (both1, x1, y1, *far1)])
    gate_grad, up_grad, *sums = input_part(
        where, rows, hidden1_all, stored[1], w_gate, w_up, total, *chunks[1], unit // 2
    )
    sums = [sums[0]] + [onward(block, rows, ahead) for ahead, block in enumerate(sums) if ahead]
    grad_gate, grad_up = weight_part(gate_grad, up_grad, inputs_all, grad_gate, grad_up, cut, unit // 2)
    grad_down = down(1, grad_down, grad_up)
    grad_inputs = sum_rows([after(sums[0], grad_down)] + sums[1:])
    return grad_inputs, grad_gate, grad_up, grad_down


def on_any(inputs, grad_out, gate_pre, up_pre, w_gate, w_up, w_down):
    inputs_all = lax.all_gather(inputs, "row", axis=0, tiled=True)
    grad_out_all = lax.all_gather(grad_out, "row", axis=0, tiled=True)
    gate_all = lax.all_gather(gate_pre, "col", axis=0, tiled=True)
    up_all = lax.all_gather(up_pre, "col", axis=0, tiled=True)
    hidden_grad = lax.psum_scatter(dot(grad_out_all, w_down, 1, 1), "col", scatter_dimension=0, tiled=True)
    gate_grad, up_grad = swiglu_back(gate_pre, up_pre, hidden_grad)
    gate_grad = lax.all_gather(gate_grad, "col", axis=0, tiled=True)
    up_grad = lax.all_gather(up_grad, "col", axis=0, tiled=True)
    grad_down = dot(hidden_of(gate_all, up_all), grad_out_all, 0, 0).astype(BF16)
    grad_gate = dot(inputs_all, gate_grad, 0, 0).astype(BF16)
    grad_up = dot(inputs_all, up_grad, 0, 0).astype(BF16)
    total = dot(gate_grad, w_gate, 1, 1) + dot(up_grad, w_up, 1, 1)
    grad_inputs = lax.psum_scatter(total, "row", scatter_dimension=0, tiled=True).astype(BF16)
    return grad_inputs, grad_gate, grad_up, grad_down


def solution(mesh):
    rows, cols = mesh.shape["row"], mesh.shape["col"]
    plan = functools.partial(on_square, rows) if (rows, cols) == (4, 8) else on_any
    placed = (
        P("row", "col"),
        P("row", "col"),
        P("col", "row"),
        P("col", "row"),
        P("col", "row"),
        P("col", "row"),
        P("row", "col"),
    )
    return jax.shard_map(
        plan,
        mesh=mesh,
        in_specs=placed,
        out_specs=(P("row", "col"), P("col", "row"), P("col", "row"), P("row", "col")),
        check_vma=False,
    )
```

```python
import functools

import jax
import jax.numpy as jnp
from jax import lax
from jax.experimental import pallas as pl
from jax.experimental.pallas import tpu as pltpu
from jax.sharding import PartitionSpec as P

BF16, F32 = jnp.bfloat16, jnp.float32
VMEM_BYTES = 56 * 1024 * 1024


def dot(a, b, a_dim, b_dim):
    return lax.dot_general(a, b, (((a_dim,), (b_dim,)), ((), ())), preferred_element_type=F32)


def logistic_of(wide):
    return 0.5 + 0.5 * jnp.tanh(0.5 * wide)


def swiglu_back(gate_pre, up_pre, hidden_grad):
    gate_wide = gate_pre.astype(F32)
    up_wide = up_pre.astype(F32)
    logistic = logistic_of(gate_wide)
    swished = gate_wide * logistic
    up_grad = (hidden_grad * swished).astype(BF16)
    gate_grad = (hidden_grad * up_wide * logistic * (1.0 + gate_wide * (1.0 - logistic))).astype(BF16)
    return gate_grad, up_grad


def hidden_of(gate_pre, up_pre):
    gate_wide = gate_pre.astype(F32)
    return (gate_wide * logistic_of(gate_wide) * up_pre.astype(F32)).astype(BF16)


def params():
    return pltpu.CompilerParams(vmem_limit_bytes=VMEM_BYTES)


def after(array, before):
    return lax.optimization_barrier((array, before))[0]


def whole_block(shape):
    return pl.BlockSpec(shape, lambda *_: (0,) * len(shape))


def swap(array, bit):
    return lax.ppermute(array, "col", [(i, i ^ bit) for i in range(8)])


def onward(array, rows, step):
    return lax.ppermute(array, "row", [(i, (i + step) % rows) for i in range(rows)])


def token_block(place, col):
    return (((place << 1) & 7) | (place >> 2)) ^ col


def place_of(block, col):
    offset = block ^ col
    return (offset >> 1) + 4 * (offset & 1)


def reorder(where, natural):
    tokens, features = natural.shape
    part = tokens // 8

    def kernel(where_ref, x, out, second):
        for place in range(8):
            start = pl.multiple_of(token_block(place, where_ref[1]) * part, part)
            rows = x[pl.ds(start, part), :]
            out[place * part : (place + 1) * part, :] = rows
            if place >= 4:
                second[(place - 4) * part : (place - 3) * part, :] = rows

    return pl.pallas_call(
        kernel,
        out_shape=[
            jax.ShapeDtypeStruct((tokens, features), BF16),
            jax.ShapeDtypeStruct((tokens // 2, features), BF16),
        ],
        in_specs=[pl.BlockSpec(memory_space=pltpu.SMEM), pl.BlockSpec(memory_space=pltpu.VMEM)],
        out_specs=[pl.BlockSpec(memory_space=pltpu.VMEM)] * 2,
        compiler_params=params(),
        name="reorder",
    )(where, natural)


def sum_rows(blocks):
    def kernel(own, *refs):
        *ins, out = refs
        total = own[...]
        for ref in ins:
            total = total + ref[...].astype(F32)
        out[...] = total.astype(BF16)

    return pl.pallas_call(
        kernel,
        out_shape=jax.ShapeDtypeStruct(blocks[0].shape, BF16),
        compiler_params=params(),
        name="sum_rows",
    )(*blocks)


def partial_hidden_grad(here, there, w_here, w_there, start, size, tile):
    tokens, features = there.shape
    part = tokens // 4

    def kernel(x, y, w, v, own, for_x, for_y, for_far):
        product = dot(x[...], w[...], 1, 1) + dot(y[...], v[...], 1, 1)
        own[...] = product[:part]
        for_x[...] = product[part : 2 * part].astype(BF16)
        for_y[...] = product[2 * part : 3 * part].astype(BF16)
        for_far[...] = product[3 * part :].astype(BF16)

    column = pl.BlockSpec((part, tile), lambda i: (0, i))
    weights = pl.BlockSpec((tile, features), lambda i: (i + start // tile, 0))
    sent = jax.ShapeDtypeStruct((part, size), BF16)
    return pl.pallas_call(
        kernel,
        grid=(size // tile,),
        in_specs=[whole_block((tokens, features))] * 2 + [weights] * 2,
        out_specs=[column] * 4,
        out_shape=[jax.ShapeDtypeStruct((part, size), F32), sent, sent, sent],
        compiler_params=params(),
        name="partial_hidden_grad",
    )(here, there, w_here, w_there)


def halved_hidden_grad(here, there, w_here, w_there, start, size, tile):
    tokens, features = there.shape
    part = tokens // 4
    half = part // 2

    def kernel(x, y, w, v, for_x, for_y, keep_x, keep_y):
        product = dot(x[...], w[...], 1, 1) + dot(y[...], v[...], 1, 1)
        own, at_x, at_y, far = [product[i * part : (i + 1) * part] for i in range(4)]
        for_x[:half] = at_x[:half].astype(BF16)
        for_x[half:] = far[:half].astype(BF16)
        for_y[:half] = at_y[half:].astype(BF16)
        for_y[half:] = far[half:].astype(BF16)
        keep_x[:half] = own[:half]
        keep_x[half:] = at_y[:half]
        keep_y[:half] = own[half:]
        keep_y[half:] = at_x[half:]

    column = pl.BlockSpec((part, tile), lambda i: (0, i))
    weights = pl.BlockSpec((tile, features), lambda i: (i + start // tile, 0))
    sent = jax.ShapeDtypeStruct((part, size), BF16)
    kept = jax.ShapeDtypeStruct((part, size), F32)
    return pl.pallas_call(
        kernel,
        grid=(size // tile,),
        in_specs=[whole_block((tokens, features))] * 2 + [weights] * 2,
        out_specs=[column] * 4,
        out_shape=[sent, sent, kept, kept],
        compiler_params=params(),
        name="halved_hidden_grad",
    )(here, there, w_here, w_there)


def pair_sum(keep_x, from_x, keep_y, from_y):
    part, size = keep_x.shape
    half = part // 2

    def kernel(a, b, c, d, for_y, for_x, own):
        upper = a[...] + b[...].astype(F32)
        lower = c[...] + d[...].astype(F32)
        own[:half] = upper[:half]
        own[half:] = lower[:half]
        for_y[...] = upper[half:].astype(BF16)
        for_x[...] = lower[half:].astype(BF16)

    sent = jax.ShapeDtypeStruct((half, size), BF16)
    return pl.pallas_call(
        kernel,
        out_shape=[sent, sent, jax.ShapeDtypeStruct((part, size), F32)],
        compiler_params=params(),
        name="pair_sum",
    )(keep_x, from_x, keep_y, from_y)


def halves_sum(own, from_y, from_x):
    half = own.shape[0] // 2

    def kernel(a, b, c, out):
        out[:half] = (a[:half] + b[...].astype(F32)).astype(BF16)
        out[half:] = (a[half:] + c[...].astype(F32)).astype(BF16)

    return pl.pallas_call(
        kernel,
        out_shape=jax.ShapeDtypeStruct(own.shape, BF16),
        compiler_params=params(),
        name="halves_sum",
    )(own, from_y, from_x)


def total_hidden_grad(own, *received):
    def kernel(a, b, c, d, out):
        out[...] = (a[...] + b[...].astype(F32) + c[...].astype(F32) + d[...].astype(F32)).astype(BF16)

    return pl.pallas_call(
        kernel,
        out_shape=jax.ShapeDtypeStruct(own.shape, BF16),
        compiler_params=params(),
        name="total_hidden_grad",
    )(own, *received)


def spread_whole(block, over_x_first):
    at_x, at_y = swap(block, 2), swap(block, 4)
    return block, at_x, at_y, swap(at_x, 4) if over_x_first else swap(at_y, 2)


def unpack(block):
    part = block.shape[0] // 8
    gate = jnp.concatenate([block[2 * i * part : (2 * i + 1) * part] for i in range(4)], axis=0)
    up = jnp.concatenate([block[(2 * i + 1) * part : (2 * i + 2) * part] for i in range(4)], axis=0)
    return gate, up


def grad_down_part(stored, grad_out_all, grad_down, hidden_units, inside, start, size, tile):
    tokens, features = grad_out_all.shape

    def kernel(p0, p1, x, *rest):
        out = rest[-1]
        hidden = jnp.concatenate([hidden_of(*unpack(p0[...])), hidden_of(*unpack(p1[...]))], axis=0)
        out[...] = dot(hidden, x[...], 0, 0).astype(BF16)

    block = pl.BlockSpec((tokens, tile), lambda i: (0, i + inside // tile))
    earlier = [] if grad_down is None else [grad_down]
    return pl.pallas_call(
        kernel,
        grid=(size // tile,),
        in_specs=[block] * 2
        + [whole_block((tokens, features))]
        + [pl.BlockSpec(memory_space=pl.ANY)] * len(earlier),
        out_specs=pl.BlockSpec((tile, features), lambda i: (i + start // tile, 0)),
        out_shape=jax.ShapeDtypeStruct((hidden_units, features), BF16),
        input_output_aliases={3: 0} if earlier else {},
        compiler_params=params(),
        name="grad_down_part",
    )(*stored, grad_out_all, *earlier)


def both_gradients(where, hidden_grad, p0, p1):
    part = hidden_grad.shape[0] // 8
    rows = []
    for place in range(8):
        start = pl.multiple_of(token_block(place, where[1]) * part, part)
        rows.append(hidden_grad[pl.ds(start, part), :])
    a0, b0 = swiglu_back(*unpack(p0[...]), jnp.concatenate(rows[:4], axis=0).astype(F32))
    a1, b1 = swiglu_back(*unpack(p1[...]), jnp.concatenate(rows[4:], axis=0).astype(F32))
    return jnp.concatenate([a0, a1], axis=0), jnp.concatenate([b0, b1], axis=0)


def first_part(where, hidden_grad, stored, inputs_all, w_gate, w_up, size, tile):
    tokens, features = inputs_all.shape

    def kernel(where_ref, h, p0, p1, x, wg, wu, grad_gate, grad_up, total):
        gate_grad, up_grad = both_gradients(where_ref, h, p0, p1)
        grad_gate[...] = dot(x[...], gate_grad, 0, 0).astype(BF16)
        grad_up[...] = dot(x[...], up_grad, 0, 0).astype(BF16)
        more = dot(gate_grad, wg[...], 1, 1) + dot(up_grad, wu[...], 1, 1)

        @pl.when(pl.program_id(0) == 0)
        def _():
            total[...] = more

        @pl.when(pl.program_id(0) > 0)
        def _():
            total[...] += more

    block = pl.BlockSpec((tokens, tile), lambda i: (0, i))
    column = pl.BlockSpec((features, tile), lambda i: (0, i))
    weights = jax.ShapeDtypeStruct(w_gate.shape, BF16)
    return pl.pallas_call(
        kernel,
        grid=(size // tile,),
        in_specs=[pl.BlockSpec(memory_space=pltpu.SMEM)]
        + [block] * 3
        + [whole_block((tokens, features)), column, column],
        out_specs=[column, column, whole_block((tokens, features))],
        out_shape=[weights, weights, jax.ShapeDtypeStruct((tokens, features), F32)],
        compiler_params=params(),
        name="first_part",
    )(where, hidden_grad, *stored, inputs_all, w_gate, w_up)


def input_part(where, rows, hidden_grad, stored, w_gate, w_up, total, start, size, tile):
    tokens, features = total.shape
    part = tokens // 8
    steps = size // tile
    strip = features // steps

    def kernel(where_ref, h, p0, p1, wg, wu, before, gate_out, up_out, *rest):
        *outs, carry = rest
        gate_grad, up_grad = both_gradients(where_ref, h, p0, p1)
        gate_out[...] = gate_grad
        up_out[...] = up_grad
        more = dot(gate_grad, wg[...], 1, 1) + dot(up_grad, wu[...], 1, 1)
        step = pl.program_id(0)

        @pl.when(step == 0)
        def _():
            carry[...] = more

        @pl.when(step > 0)
        def _():
            carry[...] += more

        carry[:, pl.ds(pl.multiple_of(step * strip, strip), strip)] += before[...]

        @pl.when(step == steps - 1)
        def _():
            row, col = where_ref[0], where_ref[1]
            for ahead, out in enumerate(outs):
                owner = lax.rem(row + ahead, rows)
                for at in range(8 // rows):
                    place = pl.multiple_of(place_of(owner * (8 // rows) + at, col) * part, part)
                    out[at * part : (at + 1) * part, :] = carry[pl.ds(place, part), :].astype(out.dtype)

    block = pl.BlockSpec((tokens, tile), lambda i: (0, i))
    column = pl.BlockSpec((features, tile), lambda i: (0, i + start // tile))
    made = jax.ShapeDtypeStruct((tokens, size), BF16)
    shape = (tokens // rows, features)
    return pl.pallas_call(
        kernel,
        grid=(steps,),
        in_specs=[pl.BlockSpec(memory_space=pltpu.SMEM)]
        + [block] * 3
        + [column, column, pl.BlockSpec((tokens, strip), lambda i: (0, i))],
        out_specs=[block, block] + [whole_block(shape)] * rows,
        out_shape=[made, made]
        + [jax.ShapeDtypeStruct(shape, F32)]
        + [jax.ShapeDtypeStruct(shape, BF16)] * (rows - 1),
        scratch_shapes=[pltpu.VMEM((tokens, features), F32)],
        compiler_params=params(),
        name="input_part",
    )(where, hidden_grad, *stored, w_gate, w_up, total)


def weight_part(gate_grad, up_grad, stored, inputs_all, grad_out_all, earlier, start, tile):
    tokens, features = inputs_all.shape
    size = gate_grad.shape[1]

    def kernel(a, b, p0, p1, x, y, *rest):
        gate_out, up_out, down_out = rest[-3:]
        gate_out[...] = dot(x[...], a[...], 0, 0).astype(BF16)
        up_out[...] = dot(x[...], b[...], 0, 0).astype(BF16)
        hidden = jnp.concatenate([hidden_of(*unpack(p0[...])), hidden_of(*unpack(p1[...]))], axis=0)
        down_out[...] = dot(hidden, y[...], 0, 0).astype(BF16)

    block = pl.BlockSpec((tokens, tile), lambda i: (0, i))
    column = pl.BlockSpec((features, tile), lambda i: (0, i + start // tile))
    row = pl.BlockSpec((tile, features), lambda i: (i + start // tile, 0))
    return pl.pallas_call(
        kernel,
        grid=(size // tile,),
        in_specs=[block] * 4
        + [whole_block((tokens, features))] * 2
        + [pl.BlockSpec(memory_space=pl.ANY)] * 3,
        out_specs=[column, column, row],
        out_shape=[jax.ShapeDtypeStruct(each.shape, BF16) for each in earlier],
        input_output_aliases={6: 0, 7: 1, 8: 2},
        compiler_params=params(),
        name="weight_part",
    )(gate_grad, up_grad, *stored, inputs_all, grad_out_all, *earlier)


def pack(pieces):
    size = pieces[0].shape[1]
    tile = size // 2
    rows = [piece.shape[0] for piece in pieces]

    def kernel(*refs):
        *ins, out = refs
        start = 0
        for ref, count in zip(ins, rows):
            out[start : start + count, :] = ref[...]
            start += count

    return pl.pallas_call(
        kernel,
        grid=(2,),
        in_specs=[pl.BlockSpec((count, tile), lambda i: (0, i)) for count in rows],
        out_specs=pl.BlockSpec((sum(rows), tile), lambda i: (0, i)),
        out_shape=jax.ShapeDtypeStruct((sum(rows), size), BF16),
        compiler_params=params(),
        name="pack",
    )(*pieces)


def both_cores(pieces):
    mine = pack(pieces)
    return mine, swap(mine, 1)


def on_square(rows, inputs, grad_out, gate_pre, up_pre, w_gate, w_up, w_down):
    hidden_units = w_gate.shape[1]
    unit = 1024
    cut = 3 * unit
    chunks = ((0, cut), (cut, hidden_units - cut))
    part = gate_pre.shape[0]
    tokens = 8 * part
    where = jnp.stack([lax.axis_index("row"), lax.axis_index("col")]).astype(jnp.int32)

    def stack(at):
        start, size = chunks[at]
        return jnp.concatenate([gate_pre[:, start : start + size], up_pre[:, start : start + size]], axis=0)

    def hidden_part(at, before):
        start, size = chunks[at]
        own, *sent = partial_hidden_grad(after(here, before), grad_out_there, w_down, w_there, start, size, unit)
        return own, sent

    def send_hidden(sent):
        return [swap(block, bits) for block, bits in zip(sent, (2, 4, 6))]

    def down(at, grad_down, before):
        start, size = chunks[at]
        return grad_down_part(
            stored[at], after(grad_out_all, before), grad_down, hidden_units, 0, start, size, unit
        )

    stored = {}
    grad_out_all = lax.all_gather(grad_out, "row", axis=0, tiled=True)
    w_there = swap(w_down, 1)
    both0, both1 = stack(0), stack(1)
    x0, y0 = swap(both0, 2), swap(both0, 4)
    x0, y0 = after(x0, both1), after(y0, both1)
    over_y, over_x = x0[:part], y0[part:]
    far0 = [swap(over_y, 4), swap(over_x, 2)]
    both1 = after(both1, (over_y, over_x))
    x1, y1 = swap(both1, 2), swap(both1, 4)
    grad_out_all, for_peer = reorder(where, after(grad_out_all, (far0, w_there)))
    here = grad_out_all
    grad_out_there = swap(for_peer, 1)
    inputs_all = lax.all_gather(after(inputs, here), "row", axis=0, tiled=True)

    own0, sent0 = hidden_part(0, here)
    got0 = send_hidden(sent0)
    for_x, for_y, keep_x, keep_y = halved_hidden_grad(
        after(here, (own0, x1, y1)), grad_out_there, w_down, w_there, *chunks[1], unit
    )
    from_x, from_y = swap(for_x, 2), swap(for_y, 4)
    stored[0] = both_cores([both0, x0, y0, *[after(piece, keep_x) for piece in far0]])
    hidden0 = total_hidden_grad(after(own0, stored[0][0]), *got0)
    hidden0_all = lax.all_gather(hidden0, "col", axis=0, tiled=True)
    x1, y1 = after(x1, hidden0), after(y1, hidden0)
    over_y, over_x = x1[:part], y1[part:]
    grad_down = down(0, None, (over_y, over_x))
    far1 = [swap(over_y, 4), swap(over_x, 2)]
    for_y, for_x, own1 = pair_sum(after(keep_x, grad_down), from_x, keep_y, from_y)
    from_y, from_x = swap(for_y, 4), swap(for_x, 2)
    inputs_all, _ = reorder(where, after(inputs_all, own1))
    hidden1 = halves_sum(after(own1, inputs_all), from_y, from_x)
    hidden1_all = lax.all_gather(hidden1, "col", axis=0, tiled=True)
    grad_gate, grad_up, total = first_part(
        where, hidden0_all, stored[0], after(inputs_all, hidden1), w_gate, w_up, cut, unit
    )
    stored[1] = both_cores([after(piece, total) for piece in (both1, x1, y1, *far1)])
    gate_grad, up_grad, *sums = input_part(
        where, rows, hidden1_all, stored[1], w_gate, w_up, total, *chunks[1], unit
    )
    sums = [sums[0]] + [onward(block, rows, ahead) for ahead, block in enumerate(sums) if ahead]
    earlier = (grad_gate, grad_up, grad_down)
    grad_gate, grad_up, grad_down = weight_part(
        gate_grad, up_grad, stored[1], inputs_all, grad_out_all, earlier, cut, unit
    )
    grad_inputs = sum_rows([after(sums[0], grad_up)] + sums[1:])
    return grad_inputs, grad_gate, grad_up, grad_down


def on_any(inputs, grad_out, gate_pre, up_pre, w_gate, w_up, w_down):
    inputs_all = lax.all_gather(inputs, "row", axis=0, tiled=True)
    grad_out_all = lax.all_gather(grad_out, "row", axis=0, tiled=True)
    gate_all = lax.all_gather(gate_pre, "col", axis=0, tiled=True)
    up_all = lax.all_gather(up_pre, "col", axis=0, tiled=True)
    hidden_grad = lax.psum_scatter(dot(grad_out_all, w_down, 1, 1), "col", scatter_dimension=0, tiled=True)
    gate_grad, up_grad = swiglu_back(gate_pre, up_pre, hidden_grad)
    gate_grad = lax.all_gather(gate_grad, "col", axis=0, tiled=True)
    up_grad = lax.all_gather(up_grad, "col", axis=0, tiled=True)
    grad_down = dot(hidden_of(gate_all, up_all), grad_out_all, 0, 0).astype(BF16)
    grad_gate = dot(inputs_all, gate_grad, 0, 0).astype(BF16)
    grad_up = dot(inputs_all, up_grad, 0, 0).astype(BF16)
    total = dot(gate_grad, w_gate, 1, 1) + dot(up_grad, w_up, 1, 1)
    grad_inputs = lax.psum_scatter(total, "row", scatter_dimension=0, tiled=True).astype(BF16)
    return grad_inputs, grad_gate, grad_up, grad_down


def solution(mesh):
    rows, cols = mesh.shape["row"], mesh.shape["col"]
    plan = functools.partial(on_square, rows) if (rows, cols) == (4, 8) else on_any
    placed = (
        P("row", "col"),
        P("row", "col"),
        P("col", "row"),
        P("col", "row"),
        P("col", "row"),
        P("col", "row"),
        P("row", "col"),
    )
    return jax.shard_map(
        plan,
        mesh=mesh,
        in_specs=placed,
        out_specs=(P("row", "col"), P("col", "row"), P("col", "row"), P("row", "col")),
        check_vma=False,
    )
```

```python
import functools

import jax
import jax.numpy as jnp
from jax import lax
from jax.experimental import pallas as pl
from jax.experimental.pallas import tpu as pltpu
from jax.sharding import PartitionSpec as P

BF16, F32 = jnp.bfloat16, jnp.float32
VMEM_BYTES = 56 * 1024 * 1024


def dot(a, b, a_dim, b_dim):
    return lax.dot_general(a, b, (((a_dim,), (b_dim,)), ((), ())), preferred_element_type=F32)


def logistic_of(wide):
    return 0.5 + 0.5 * jnp.tanh(0.5 * wide)


def swiglu_back(gate_pre, up_pre, hidden_grad):
    gate_wide = gate_pre.astype(F32)
    up_wide = up_pre.astype(F32)
    logistic = logistic_of(gate_wide)
    swished = gate_wide * logistic
    up_grad = (hidden_grad * swished).astype(BF16)
    gate_grad = (hidden_grad * up_wide * logistic * (1.0 + gate_wide * (1.0 - logistic))).astype(BF16)
    return gate_grad, up_grad


def hidden_of(gate_pre, up_pre):
    gate_wide = gate_pre.astype(F32)
    return (gate_wide * logistic_of(gate_wide) * up_pre.astype(F32)).astype(BF16)


def params():
    return pltpu.CompilerParams(vmem_limit_bytes=VMEM_BYTES)


def after(array, before):
    return lax.optimization_barrier((array, before))[0]


def whole_block(shape):
    return pl.BlockSpec(shape, lambda *_: (0,) * len(shape))


def swap(array, bit):
    return lax.ppermute(array, "col", [(i, i ^ bit) for i in range(8)])


def onward(array, rows, step):
    return lax.ppermute(array, "row", [(i, (i + step) % rows) for i in range(rows)])


def token_block(place, col):
    return (((place << 1) & 7) | (place >> 2)) ^ col


def place_of(block, col):
    offset = block ^ col
    return (offset >> 1) + 4 * (offset & 1)


def reorder(where, natural):
    tokens, features = natural.shape
    part = tokens // 8

    def kernel(where_ref, x, out, second):
        for place in range(8):
            start = pl.multiple_of(token_block(place, where_ref[1]) * part, part)
            rows = x[pl.ds(start, part), :]
            out[place * part : (place + 1) * part, :] = rows
            if place >= 4:
                second[(place - 4) * part : (place - 3) * part, :] = rows

    return pl.pallas_call(
        kernel,
        out_shape=[
            jax.ShapeDtypeStruct((tokens, features), BF16),
            jax.ShapeDtypeStruct((tokens // 2, features), BF16),
        ],
        in_specs=[pl.BlockSpec(memory_space=pltpu.SMEM), pl.BlockSpec(memory_space=pltpu.VMEM)],
        out_specs=[pl.BlockSpec(memory_space=pltpu.VMEM)] * 2,
        compiler_params=params(),
        name="reorder",
    )(where, natural)


def sum_rows(blocks):
    def kernel(own, *refs):
        *ins, out = refs
        total = own[...]
        for ref in ins:
            total = total + ref[...].astype(F32)
        out[...] = total.astype(BF16)

    return pl.pallas_call(
        kernel,
        out_shape=jax.ShapeDtypeStruct(blocks[0].shape, BF16),
        compiler_params=params(),
        name="sum_rows",
    )(*blocks)


def partial_hidden_grad(here, there, w_here, w_there, start, size, tile):
    tokens, features = there.shape
    part = tokens // 4

    def kernel(x, y, w, v, own, for_x, for_y, for_far):
        product = dot(x[...], w[...], 1, 1) + dot(y[...], v[...], 1, 1)
        own[...] = product[:part]
        for_x[...] = product[part : 2 * part].astype(BF16)
        for_y[...] = product[2 * part : 3 * part].astype(BF16)
        for_far[...] = product[3 * part :].astype(BF16)

    column = pl.BlockSpec((part, tile), lambda i: (0, i))
    weights = pl.BlockSpec((tile, features), lambda i: (i + start // tile, 0))
    sent = jax.ShapeDtypeStruct((part, size), BF16)
    return pl.pallas_call(
        kernel,
        grid=(size // tile,),
        in_specs=[whole_block((tokens, features))] * 2 + [weights] * 2,
        out_specs=[column] * 4,
        out_shape=[jax.ShapeDtypeStruct((part, size), F32), sent, sent, sent],
        compiler_params=params(),
        name="partial_hidden_grad",
    )(here, there, w_here, w_there)


def halved_hidden_grad(here, there, w_here, w_there, start, size, tile):
    tokens, features = there.shape
    part = tokens // 4
    half = part // 2

    def kernel(x, y, w, v, for_x, for_y, keep_x, keep_y):
        product = dot(x[...], w[...], 1, 1) + dot(y[...], v[...], 1, 1)
        own, at_x, at_y, far = [product[i * part : (i + 1) * part] for i in range(4)]
        for_x[:half] = at_x[:half].astype(BF16)
        for_x[half:] = far[:half].astype(BF16)
        for_y[:half] = at_y[half:].astype(BF16)
        for_y[half:] = far[half:].astype(BF16)
        keep_x[:half] = own[:half]
        keep_x[half:] = at_y[:half]
        keep_y[:half] = own[half:]
        keep_y[half:] = at_x[half:]

    column = pl.BlockSpec((part, tile), lambda i: (0, i))
    weights = pl.BlockSpec((tile, features), lambda i: (i + start // tile, 0))
    sent = jax.ShapeDtypeStruct((part, size), BF16)
    kept = jax.ShapeDtypeStruct((part, size), F32)
    return pl.pallas_call(
        kernel,
        grid=(size // tile,),
        in_specs=[whole_block((tokens, features))] * 2 + [weights] * 2,
        out_specs=[column] * 4,
        out_shape=[sent, sent, kept, kept],
        compiler_params=params(),
        name="halved_hidden_grad",
    )(here, there, w_here, w_there)


def pair_sum(keep_x, from_x, keep_y, from_y):
    part, size = keep_x.shape
    half = part // 2

    def kernel(a, b, c, d, for_y, for_x, own):
        upper = a[...] + b[...].astype(F32)
        lower = c[...] + d[...].astype(F32)
        own[:half] = upper[:half]
        own[half:] = lower[:half]
        for_y[...] = upper[half:].astype(BF16)
        for_x[...] = lower[half:].astype(BF16)

    sent = jax.ShapeDtypeStruct((half, size), BF16)
    return pl.pallas_call(
        kernel,
        out_shape=[sent, sent, jax.ShapeDtypeStruct((part, size), F32)],
        compiler_params=params(),
        name="pair_sum",
    )(keep_x, from_x, keep_y, from_y)


def halves_sum(own, from_y, from_x):
    half = own.shape[0] // 2

    def kernel(a, b, c, out):
        out[:half] = (a[:half] + b[...].astype(F32)).astype(BF16)
        out[half:] = (a[half:] + c[...].astype(F32)).astype(BF16)

    return pl.pallas_call(
        kernel,
        out_shape=jax.ShapeDtypeStruct(own.shape, BF16),
        compiler_params=params(),
        name="halves_sum",
    )(own, from_y, from_x)


def total_hidden_grad(own, *received):
    def kernel(a, b, c, d, out):
        out[...] = (a[...] + b[...].astype(F32) + c[...].astype(F32) + d[...].astype(F32)).astype(BF16)

    return pl.pallas_call(
        kernel,
        out_shape=jax.ShapeDtypeStruct(own.shape, BF16),
        compiler_params=params(),
        name="total_hidden_grad",
    )(own, *received)


def spread_whole(block, over_x_first):
    at_x, at_y = swap(block, 2), swap(block, 4)
    return block, at_x, at_y, swap(at_x, 4) if over_x_first else swap(at_y, 2)


def unpack(block):
    part = block.shape[0] // 8
    gate = jnp.concatenate([block[2 * i * part : (2 * i + 1) * part] for i in range(4)], axis=0)
    up = jnp.concatenate([block[(2 * i + 1) * part : (2 * i + 2) * part] for i in range(4)], axis=0)
    return gate, up


def grad_down_part(stored, grad_out_all, grad_down, hidden_units, inside, start, size, tile):
    tokens, features = grad_out_all.shape

    def kernel(p0, p1, x, *rest):
        out = rest[-1]
        hidden = jnp.concatenate([hidden_of(*unpack(p0[...])), hidden_of(*unpack(p1[...]))], axis=0)
        out[...] = dot(hidden, x[...], 0, 0).astype(BF16)

    block = pl.BlockSpec((tokens, tile), lambda i: (0, i + inside // tile))
    earlier = [] if grad_down is None else [grad_down]
    return pl.pallas_call(
        kernel,
        grid=(size // tile,),
        in_specs=[block] * 2
        + [whole_block((tokens, features))]
        + [pl.BlockSpec(memory_space=pl.ANY)] * len(earlier),
        out_specs=pl.BlockSpec((tile, features), lambda i: (i + start // tile, 0)),
        out_shape=jax.ShapeDtypeStruct((hidden_units, features), BF16),
        input_output_aliases={3: 0} if earlier else {},
        compiler_params=params(),
        name="grad_down_part",
    )(*stored, grad_out_all, *earlier)


def both_gradients(where, hidden_grad, p0, p1):
    part = hidden_grad.shape[0] // 8
    rows = []
    for place in range(8):
        start = pl.multiple_of(token_block(place, where[1]) * part, part)
        rows.append(hidden_grad[pl.ds(start, part), :])
    a0, b0 = swiglu_back(*unpack(p0[...]), jnp.concatenate(rows[:4], axis=0).astype(F32))
    a1, b1 = swiglu_back(*unpack(p1[...]), jnp.concatenate(rows[4:], axis=0).astype(F32))
    return jnp.concatenate([a0, a1], axis=0), jnp.concatenate([b0, b1], axis=0)


def first_part(where, hidden_grad, stored, inputs_all, w_gate, w_up, size, tile):
    tokens, features = inputs_all.shape

    def kernel(where_ref, h, p0, p1, x, wg, wu, grad_gate, grad_up, total):
        gate_grad, up_grad = both_gradients(where_ref, h, p0, p1)
        grad_gate[...] = dot(x[...], gate_grad, 0, 0).astype(BF16)
        grad_up[...] = dot(x[...], up_grad, 0, 0).astype(BF16)
        more = dot(gate_grad, wg[...], 1, 1) + dot(up_grad, wu[...], 1, 1)

        @pl.when(pl.program_id(0) == 0)
        def _():
            total[...] = more

        @pl.when(pl.program_id(0) > 0)
        def _():
            total[...] += more

    block = pl.BlockSpec((tokens, tile), lambda i: (0, i))
    column = pl.BlockSpec((features, tile), lambda i: (0, i))
    weights = jax.ShapeDtypeStruct(w_gate.shape, BF16)
    return pl.pallas_call(
        kernel,
        grid=(size // tile,),
        in_specs=[pl.BlockSpec(memory_space=pltpu.SMEM)]
        + [block] * 3
        + [whole_block((tokens, features)), column, column],
        out_specs=[column, column, whole_block((tokens, features))],
        out_shape=[weights, weights, jax.ShapeDtypeStruct((tokens, features), F32)],
        compiler_params=params(),
        name="first_part",
    )(where, hidden_grad, *stored, inputs_all, w_gate, w_up)


def input_part(where, rows, hidden_grad, stored, w_gate, w_up, total, start, size, tile):
    tokens, features = total.shape
    part = tokens // 8
    steps = size // tile
    strip = features // steps

    def kernel(where_ref, h, p0, p1, wg, wu, before, gate_out, up_out, *rest):
        *outs, carry = rest
        gate_grad, up_grad = both_gradients(where_ref, h, p0, p1)
        gate_out[...] = gate_grad
        up_out[...] = up_grad
        more = dot(gate_grad, wg[...], 1, 1) + dot(up_grad, wu[...], 1, 1)
        step = pl.program_id(0)

        @pl.when(step == 0)
        def _():
            carry[...] = more

        @pl.when(step > 0)
        def _():
            carry[...] += more

        carry[:, pl.ds(pl.multiple_of(step * strip, strip), strip)] += before[...]

        @pl.when(step == steps - 1)
        def _():
            row, col = where_ref[0], where_ref[1]
            for ahead, out in enumerate(outs):
                owner = lax.rem(row + ahead, rows)
                for at in range(8 // rows):
                    place = pl.multiple_of(place_of(owner * (8 // rows) + at, col) * part, part)
                    out[at * part : (at + 1) * part, :] = carry[pl.ds(place, part), :].astype(out.dtype)

    block = pl.BlockSpec((tokens, tile), lambda i: (0, i))
    column = pl.BlockSpec((features, tile), lambda i: (0, i + start // tile))
    made = jax.ShapeDtypeStruct((tokens, size), BF16)
    shape = (tokens // rows, features)
    return pl.pallas_call(
        kernel,
        grid=(steps,),
        in_specs=[pl.BlockSpec(memory_space=pltpu.SMEM)]
        + [block] * 3
        + [column, column, pl.BlockSpec((tokens, strip), lambda i: (0, i))],
        out_specs=[block, block] + [whole_block(shape)] * rows,
        out_shape=[made, made]
        + [jax.ShapeDtypeStruct(shape, F32)]
        + [jax.ShapeDtypeStruct(shape, BF16)] * (rows - 1),
        scratch_shapes=[pltpu.VMEM((tokens, features), F32)],
        compiler_params=params(),
        name="input_part",
    )(where, hidden_grad, *stored, w_gate, w_up, total)


def weight_part(gate_grad, up_grad, stored, inputs_all, grad_out_all, earlier, start, tile):
    tokens, features = inputs_all.shape
    size = gate_grad.shape[1]

    def kernel(a, b, p0, p1, x, y, *rest):
        gate_out, up_out, down_out = rest[-3:]
        gate_out[...] = dot(x[...], a[...], 0, 0).astype(BF16)
        up_out[...] = dot(x[...], b[...], 0, 0).astype(BF16)
        hidden = jnp.concatenate([hidden_of(*unpack(p0[...])), hidden_of(*unpack(p1[...]))], axis=0)
        down_out[...] = dot(hidden, y[...], 0, 0).astype(BF16)

    block = pl.BlockSpec((tokens, tile), lambda i: (0, i))
    column = pl.BlockSpec((features, tile), lambda i: (0, i + start // tile))
    row = pl.BlockSpec((tile, features), lambda i: (i + start // tile, 0))
    return pl.pallas_call(
        kernel,
        grid=(size // tile,),
        in_specs=[block] * 4
        + [whole_block((tokens, features))] * 2
        + [pl.BlockSpec(memory_space=pl.ANY)] * 3,
        out_specs=[column, column, row],
        out_shape=[jax.ShapeDtypeStruct(each.shape, BF16) for each in earlier],
        input_output_aliases={6: 0, 7: 1, 8: 2},
        compiler_params=params(),
        name="weight_part",
    )(gate_grad, up_grad, *stored, inputs_all, grad_out_all, *earlier)


def pack(pieces):
    size = pieces[0].shape[1]
    tile = size // 2
    rows = [piece.shape[0] for piece in pieces]

    def kernel(*refs):
        *ins, out = refs
        start = 0
        for ref, count in zip(ins, rows):
            out[start : start + count, :] = ref[...]
            start += count

    return pl.pallas_call(
        kernel,
        grid=(2,),
        in_specs=[pl.BlockSpec((count, tile), lambda i: (0, i)) for count in rows],
        out_specs=pl.BlockSpec((sum(rows), tile), lambda i: (0, i)),
        out_shape=jax.ShapeDtypeStruct((sum(rows), size), BF16),
        compiler_params=params(),
        name="pack",
    )(*pieces)


def both_cores(pieces):
    mine = pack(pieces)
    return mine, swap(mine, 1)


def on_square(rows, inputs, grad_out, gate_pre, up_pre, w_gate, w_up, w_down):
    hidden_units = w_gate.shape[1]
    unit = 1024
    cut = 3 * unit
    chunks = ((0, cut), (cut, hidden_units - cut))
    part = gate_pre.shape[0]
    tokens = 8 * part
    where = jnp.stack([lax.axis_index("row"), lax.axis_index("col")]).astype(jnp.int32)

    def stack(at):
        start, size = chunks[at]
        return jnp.concatenate([gate_pre[:, start : start + size], up_pre[:, start : start + size]], axis=0)

    def hidden_part(at, before):
        start, size = chunks[at]
        own, *sent = partial_hidden_grad(after(here, before), grad_out_there, w_down, w_there, start, size, unit)
        return own, sent

    def send_hidden(sent):
        return [swap(block, bits) for block, bits in zip(sent, (2, 4, 6))]

    def down(at, grad_down, before):
        start, size = chunks[at]
        return grad_down_part(
            stored[at], after(grad_out_all, before), grad_down, hidden_units, 0, start, size, unit
        )

    stored = {}
    grad_out_all = lax.all_gather(grad_out, "row", axis=0, tiled=True)
    w_there = swap(w_down, 1)
    both0, both1 = stack(0), stack(1)
    x0, y0 = swap(both0, 2), swap(both0, 4)
    x0, y0 = after(x0, both1), after(y0, both1)
    over_y, over_x = x0[:part], y0[part:]
    far0 = [swap(over_y, 4), swap(over_x, 2)]
    both1 = after(both1, (over_y, over_x))
    x1, y1 = swap(both1, 2), swap(both1, 4)
    grad_out_all, for_peer = reorder(where, after(grad_out_all, (far0, w_there)))
    here = grad_out_all
    grad_out_there = swap(for_peer, 1)
    inputs_all = lax.all_gather(after(inputs, here), "row", axis=0, tiled=True)

    own0, sent0 = hidden_part(0, here)
    got0 = send_hidden(sent0)
    for_x, for_y, keep_x, keep_y = halved_hidden_grad(
        after(here, (own0, x1, y1)), grad_out_there, w_down, w_there, *chunks[1], unit
    )
    from_x, from_y = swap(for_x, 2), swap(for_y, 4)
    stored[0] = both_cores([both0, x0, y0, *[after(piece, keep_x) for piece in far0]])
    hidden0 = total_hidden_grad(after(own0, stored[0][0]), *got0)
    hidden0_all = lax.all_gather(hidden0, "col", axis=0, tiled=True)
    x1, y1 = after(x1, hidden0), after(y1, hidden0)
    over_y, over_x = x1[:part], y1[part:]
    inputs_all, _ = reorder(where, after(inputs_all, (over_y, over_x)))
    for_y, for_x, own1 = pair_sum(after(keep_x, inputs_all), from_x, keep_y, from_y)
    from_y, from_x = swap(for_y, 4), swap(for_x, 2)
    far1 = [swap(after(over_y, own1), 4), swap(after(over_x, own1), 2)]
    grad_down = down(0, None, own1)
    hidden1 = halves_sum(after(own1, grad_down), from_y, from_x)
    hidden1_all = lax.all_gather(hidden1, "col", axis=0, tiled=True)
    grad_gate, grad_up, total = first_part(
        where, hidden0_all, stored[0], after(inputs_all, hidden1), w_gate, w_up, cut, unit
    )
    stored[1] = both_cores([after(piece, total) for piece in (both1, x1, y1, *far1)])
    gate_grad, up_grad, *sums = input_part(
        where, rows, hidden1_all, stored[1], w_gate, w_up, total, *chunks[1], unit
    )
    sums = [sums[0]] + [onward(block, rows, ahead) for ahead, block in enumerate(sums) if ahead]
    earlier = (grad_gate, grad_up, grad_down)
    grad_gate, grad_up, grad_down = weight_part(
        gate_grad, up_grad, stored[1], inputs_all, grad_out_all, earlier, cut, unit
    )
    grad_inputs = sum_rows([after(sums[0], grad_up)] + sums[1:])
    return grad_inputs, grad_gate, grad_up, grad_down


def on_any(inputs, grad_out, gate_pre, up_pre, w_gate, w_up, w_down):
    inputs_all = lax.all_gather(inputs, "row", axis=0, tiled=True)
    grad_out_all = lax.all_gather(grad_out, "row", axis=0, tiled=True)
    gate_all = lax.all_gather(gate_pre, "col", axis=0, tiled=True)
    up_all = lax.all_gather(up_pre, "col", axis=0, tiled=True)
    hidden_grad = lax.psum_scatter(dot(grad_out_all, w_down, 1, 1), "col", scatter_dimension=0, tiled=True)
    gate_grad, up_grad = swiglu_back(gate_pre, up_pre, hidden_grad)
    gate_grad = lax.all_gather(gate_grad, "col", axis=0, tiled=True)
    up_grad = lax.all_gather(up_grad, "col", axis=0, tiled=True)
    grad_down = dot(hidden_of(gate_all, up_all), grad_out_all, 0, 0).astype(BF16)
    grad_gate = dot(inputs_all, gate_grad, 0, 0).astype(BF16)
    grad_up = dot(inputs_all, up_grad, 0, 0).astype(BF16)
    total = dot(gate_grad, w_gate, 1, 1) + dot(up_grad, w_up, 1, 1)
    grad_inputs = lax.psum_scatter(total, "row", scatter_dimension=0, tiled=True).astype(BF16)
    return grad_inputs, grad_gate, grad_up, grad_down


def solution(mesh):
    rows, cols = mesh.shape["row"], mesh.shape["col"]
    plan = functools.partial(on_square, rows) if (rows, cols) == (4, 8) else on_any
    placed = (
        P("row", "col"),
        P("row", "col"),
        P("col", "row"),
        P("col", "row"),
        P("col", "row"),
        P("col", "row"),
        P("row", "col"),
    )
    return jax.shard_map(
        plan,
        mesh=mesh,
        in_specs=placed,
        out_specs=(P("row", "col"), P("col", "row"), P("col", "row"), P("row", "col")),
        check_vma=False,
    )
```

```python
import functools

import jax
import jax.numpy as jnp
from jax import lax
from jax.experimental import pallas as pl
from jax.experimental.pallas import tpu as pltpu
from jax.sharding import PartitionSpec as P

BF16, F32 = jnp.bfloat16, jnp.float32
VMEM_BYTES = 56 * 1024 * 1024


def dot(a, b, a_dim, b_dim):
    return lax.dot_general(a, b, (((a_dim,), (b_dim,)), ((), ())), preferred_element_type=F32)


def logistic_of(wide):
    return 0.5 + 0.5 * jnp.tanh(0.5 * wide)


def swiglu_back(gate_pre, up_pre, hidden_grad):
    gate_wide = gate_pre.astype(F32)
    up_wide = up_pre.astype(F32)
    logistic = logistic_of(gate_wide)
    swished = gate_wide * logistic
    up_grad = (hidden_grad * swished).astype(BF16)
    gate_grad = (hidden_grad * up_wide * logistic * (1.0 + gate_wide * (1.0 - logistic))).astype(BF16)
    return gate_grad, up_grad


def hidden_of(gate_pre, up_pre):
    gate_wide = gate_pre.astype(F32)
    return (gate_wide * logistic_of(gate_wide) * up_pre.astype(F32)).astype(BF16)


def params():
    return pltpu.CompilerParams(vmem_limit_bytes=VMEM_BYTES)


def after(array, before):
    return lax.optimization_barrier((array, before))[0]


def whole_block(shape):
    return pl.BlockSpec(shape, lambda *_: (0,) * len(shape))


def swap(array, bit):
    return lax.ppermute(array, "col", [(i, i ^ bit) for i in range(8)])


def onward(array, rows, step):
    return lax.ppermute(array, "row", [(i, (i + step) % rows) for i in range(rows)])


def token_block(place, col):
    return (((place << 1) & 7) | (place >> 2)) ^ col


def place_of(block, col):
    offset = block ^ col
    return (offset >> 1) + 4 * (offset & 1)


def reorder(where, natural):
    tokens, features = natural.shape
    part = tokens // 8

    def kernel(where_ref, x, out, second):
        for place in range(8):
            start = pl.multiple_of(token_block(place, where_ref[1]) * part, part)
            rows = x[pl.ds(start, part), :]
            out[place * part : (place + 1) * part, :] = rows
            if place >= 4:
                second[(place - 4) * part : (place - 3) * part, :] = rows

    return pl.pallas_call(
        kernel,
        out_shape=[
            jax.ShapeDtypeStruct((tokens, features), BF16),
            jax.ShapeDtypeStruct((tokens // 2, features), BF16),
        ],
        in_specs=[pl.BlockSpec(memory_space=pltpu.SMEM), pl.BlockSpec(memory_space=pltpu.VMEM)],
        out_specs=[pl.BlockSpec(memory_space=pltpu.VMEM)] * 2,
        compiler_params=params(),
        name="reorder",
    )(where, natural)


def sum_rows(blocks):
    total = blocks[0]
    for block in blocks[1:]:
        total = total + block.astype(F32)
    return total.astype(BF16)


def partial_hidden_grad(here, there, w_here, w_there, start, size, tile):
    tokens, features = there.shape
    part = tokens // 4

    def kernel(x, y, w, v, own, for_x, for_y, for_far):
        product = dot(x[...], w[...], 1, 1) + dot(y[...], v[...], 1, 1)
        own[...] = product[:part]
        for_x[...] = product[part : 2 * part].astype(BF16)
        for_y[...] = product[2 * part : 3 * part].astype(BF16)
        for_far[...] = product[3 * part :].astype(BF16)

    column = pl.BlockSpec((part, tile), lambda i: (0, i))
    weights = pl.BlockSpec((tile, features), lambda i: (i + start // tile, 0))
    sent = jax.ShapeDtypeStruct((part, size), BF16)
    return pl.pallas_call(
        kernel,
        grid=(size // tile,),
        in_specs=[whole_block((tokens, features))] * 2 + [weights] * 2,
        out_specs=[column] * 4,
        out_shape=[jax.ShapeDtypeStruct((part, size), F32), sent, sent, sent],
        compiler_params=params(),
        name="partial_hidden_grad",
    )(here, there, w_here, w_there)


def halved_hidden_grad(here, there, w_here, w_there, start, size, tile):
    tokens, features = there.shape
    part = tokens // 4
    half = part // 2

    def kernel(x, y, w, v, for_x, for_y, keep_x, keep_y):
        product = dot(x[...], w[...], 1, 1) + dot(y[...], v[...], 1, 1)
        own, at_x, at_y, far = [product[i * part : (i + 1) * part] for i in range(4)]
        for_x[:half] = at_x[:half].astype(BF16)
        for_x[half:] = far[:half].astype(BF16)
        for_y[:half] = at_y[half:].astype(BF16)
        for_y[half:] = far[half:].astype(BF16)
        keep_x[:half] = own[:half]
        keep_x[half:] = at_y[:half]
        keep_y[:half] = own[half:]
        keep_y[half:] = at_x[half:]

    column = pl.BlockSpec((part, tile), lambda i: (0, i))
    weights = pl.BlockSpec((tile, features), lambda i: (i + start // tile, 0))
    sent = jax.ShapeDtypeStruct((part, size), BF16)
    kept = jax.ShapeDtypeStruct((part, size), F32)
    return pl.pallas_call(
        kernel,
        grid=(size // tile,),
        in_specs=[whole_block((tokens, features))] * 2 + [weights] * 2,
        out_specs=[column] * 4,
        out_shape=[sent, sent, kept, kept],
        compiler_params=params(),
        name="halved_hidden_grad",
    )(here, there, w_here, w_there)


def pair_sum(keep_x, from_x, keep_y, from_y):
    part, size = keep_x.shape
    half = part // 2

    def kernel(a, b, c, d, for_y, for_x, own):
        upper = a[...] + b[...].astype(F32)
        lower = c[...] + d[...].astype(F32)
        own[:half] = upper[:half]
        own[half:] = lower[:half]
        for_y[...] = upper[half:].astype(BF16)
        for_x[...] = lower[half:].astype(BF16)

    sent = jax.ShapeDtypeStruct((half, size), BF16)
    return pl.pallas_call(
        kernel,
        out_shape=[sent, sent, jax.ShapeDtypeStruct((part, size), F32)],
        compiler_params=params(),
        name="pair_sum",
    )(keep_x, from_x, keep_y, from_y)


def halves_sum(own, from_y, from_x):
    half = own.shape[0] // 2

    def kernel(a, b, c, out):
        out[:half] = (a[:half] + b[...].astype(F32)).astype(BF16)
        out[half:] = (a[half:] + c[...].astype(F32)).astype(BF16)

    return pl.pallas_call(
        kernel,
        out_shape=jax.ShapeDtypeStruct(own.shape, BF16),
        compiler_params=params(),
        name="halves_sum",
    )(own, from_y, from_x)


def total_hidden_grad(own, *received):
    return sum_rows([own, *received])


def spread_whole(block, over_x_first):
    at_x, at_y = swap(block, 2), swap(block, 4)
    return block, at_x, at_y, swap(at_x, 4) if over_x_first else swap(at_y, 2)


def unpack(block):
    part = block.shape[0] // 8
    gate = jnp.concatenate([block[2 * i * part : (2 * i + 1) * part] for i in range(4)], axis=0)
    up = jnp.concatenate([block[(2 * i + 1) * part : (2 * i + 2) * part] for i in range(4)], axis=0)
    return gate, up


def grad_down_part(stored, grad_out_all, grad_down, hidden_units, inside, start, size, tile):
    tokens, features = grad_out_all.shape

    def kernel(p0, p1, x, *rest):
        out = rest[-1]
        hidden = jnp.concatenate([hidden_of(*unpack(p0[...])), hidden_of(*unpack(p1[...]))], axis=0)
        out[...] = dot(hidden, x[...], 0, 0).astype(BF16)

    block = pl.BlockSpec((tokens, tile), lambda i: (0, i + inside // tile))
    earlier = [] if grad_down is None else [grad_down]
    return pl.pallas_call(
        kernel,
        grid=(size // tile,),
        in_specs=[block] * 2
        + [whole_block((tokens, features))]
        + [pl.BlockSpec(memory_space=pl.ANY)] * len(earlier),
        out_specs=pl.BlockSpec((tile, features), lambda i: (i + start // tile, 0)),
        out_shape=jax.ShapeDtypeStruct((hidden_units, features), BF16),
        input_output_aliases={3: 0} if earlier else {},
        compiler_params=params(),
        name="grad_down_part",
    )(*stored, grad_out_all, *earlier)


def both_gradients(where, hidden_grad, p0, p1):
    part = hidden_grad.shape[0] // 8
    rows = []
    for place in range(8):
        start = pl.multiple_of(token_block(place, where[1]) * part, part)
        rows.append(hidden_grad[pl.ds(start, part), :])
    a0, b0 = swiglu_back(*unpack(p0[...]), jnp.concatenate(rows[:4], axis=0).astype(F32))
    a1, b1 = swiglu_back(*unpack(p1[...]), jnp.concatenate(rows[4:], axis=0).astype(F32))
    return jnp.concatenate([a0, a1], axis=0), jnp.concatenate([b0, b1], axis=0)


def first_part(where, hidden_grad, stored, inputs_all, w_gate, w_up, size, tile):
    tokens, features = inputs_all.shape

    def kernel(where_ref, h, p0, p1, x, wg, wu, grad_gate, grad_up, total):
        gate_grad, up_grad = both_gradients(where_ref, h, p0, p1)
        grad_gate[...] = dot(x[...], gate_grad, 0, 0).astype(BF16)
        grad_up[...] = dot(x[...], up_grad, 0, 0).astype(BF16)
        more = dot(gate_grad, wg[...], 1, 1) + dot(up_grad, wu[...], 1, 1)

        @pl.when(pl.program_id(0) == 0)
        def _():
            total[...] = more

        @pl.when(pl.program_id(0) > 0)
        def _():
            total[...] += more

    block = pl.BlockSpec((tokens, tile), lambda i: (0, i))
    column = pl.BlockSpec((features, tile), lambda i: (0, i))
    weights = jax.ShapeDtypeStruct(w_gate.shape, BF16)
    return pl.pallas_call(
        kernel,
        grid=(size // tile,),
        in_specs=[pl.BlockSpec(memory_space=pltpu.SMEM)]
        + [block] * 3
        + [whole_block((tokens, features)), column, column],
        out_specs=[column, column, whole_block((tokens, features))],
        out_shape=[weights, weights, jax.ShapeDtypeStruct((tokens, features), F32)],
        compiler_params=params(),
        name="first_part",
    )(where, hidden_grad, *stored, inputs_all, w_gate, w_up)


def input_part(where, rows, hidden_grad, stored, w_gate, w_up, total, start, size, tile):
    tokens, features = total.shape
    part = tokens // 8
    steps = size // tile
    strip = features // steps

    def kernel(where_ref, h, p0, p1, wg, wu, before, gate_out, up_out, *rest):
        *outs, carry = rest
        gate_grad, up_grad = both_gradients(where_ref, h, p0, p1)
        gate_out[...] = gate_grad
        up_out[...] = up_grad
        more = dot(gate_grad, wg[...], 1, 1) + dot(up_grad, wu[...], 1, 1)
        step = pl.program_id(0)

        @pl.when(step == 0)
        def _():
            carry[...] = more

        @pl.when(step > 0)
        def _():
            carry[...] += more

        carry[:, pl.ds(pl.multiple_of(step * strip, strip), strip)] += before[...]

        @pl.when(step == steps - 1)
        def _():
            row, col = where_ref[0], where_ref[1]
            for ahead, out in enumerate(outs):
                owner = lax.rem(row + ahead, rows)
                for at in range(8 // rows):
                    place = pl.multiple_of(place_of(owner * (8 // rows) + at, col) * part, part)
                    out[at * part : (at + 1) * part, :] = carry[pl.ds(place, part), :].astype(out.dtype)

    block = pl.BlockSpec((tokens, tile), lambda i: (0, i))
    column = pl.BlockSpec((features, tile), lambda i: (0, i + start // tile))
    made = jax.ShapeDtypeStruct((tokens, size), BF16)
    shape = (tokens // rows, features)
    return pl.pallas_call(
        kernel,
        grid=(steps,),
        in_specs=[pl.BlockSpec(memory_space=pltpu.SMEM)]
        + [block] * 3
        + [column, column, pl.BlockSpec((tokens, strip), lambda i: (0, i))],
        out_specs=[block, block] + [whole_block(shape)] * rows,
        out_shape=[made, made]
        + [jax.ShapeDtypeStruct(shape, F32)]
        + [jax.ShapeDtypeStruct(shape, BF16)] * (rows - 1),
        scratch_shapes=[pltpu.VMEM((tokens, features), F32)],
        compiler_params=params(),
        name="input_part",
    )(where, hidden_grad, *stored, w_gate, w_up, total)


def weight_part(gate_grad, up_grad, stored, inputs_all, grad_out_all, earlier, start, tile):
    tokens, features = inputs_all.shape
    size = gate_grad.shape[1]

    def kernel(a, b, p0, p1, x, y, *rest):
        gate_out, up_out, down_out = rest[-3:]
        gate_out[...] = dot(x[...], a[...], 0, 0).astype(BF16)
        up_out[...] = dot(x[...], b[...], 0, 0).astype(BF16)
        hidden = jnp.concatenate([hidden_of(*unpack(p0[...])), hidden_of(*unpack(p1[...]))], axis=0)
        down_out[...] = dot(hidden, y[...], 0, 0).astype(BF16)

    block = pl.BlockSpec((tokens, tile), lambda i: (0, i))
    column = pl.BlockSpec((features, tile), lambda i: (0, i + start // tile))
    row = pl.BlockSpec((tile, features), lambda i: (i + start // tile, 0))
    return pl.pallas_call(
        kernel,
        grid=(size // tile,),
        in_specs=[block] * 4
        + [whole_block((tokens, features))] * 2
        + [pl.BlockSpec(memory_space=pl.ANY)] * 3,
        out_specs=[column, column, row],
        out_shape=[jax.ShapeDtypeStruct(each.shape, BF16) for each in earlier],
        input_output_aliases={6: 0, 7: 1, 8: 2},
        compiler_params=params(),
        name="weight_part",
    )(gate_grad, up_grad, *stored, inputs_all, grad_out_all, *earlier)


def pack(pieces):
    size = pieces[0].shape[1]
    tile = size // 2
    rows = [piece.shape[0] for piece in pieces]

    def kernel(*refs):
        *ins, out = refs
        start = 0
        for ref, count in zip(ins, rows):
            out[start : start + count, :] = ref[...]
            start += count

    return pl.pallas_call(
        kernel,
        grid=(2,),
        in_specs=[pl.BlockSpec((count, tile), lambda i: (0, i)) for count in rows],
        out_specs=pl.BlockSpec((sum(rows), tile), lambda i: (0, i)),
        out_shape=jax.ShapeDtypeStruct((sum(rows), size), BF16),
        compiler_params=params(),
        name="pack",
    )(*pieces)


def both_cores(pieces):
    mine = pack(pieces)
    return mine, swap(mine, 1)


def on_square(rows, inputs, grad_out, gate_pre, up_pre, w_gate, w_up, w_down):
    hidden_units = w_gate.shape[1]
    unit = 1024
    cut = 3 * unit
    chunks = ((0, cut), (cut, hidden_units - cut))
    part = gate_pre.shape[0]
    tokens = 8 * part
    where = jnp.stack([lax.axis_index("row"), lax.axis_index("col")]).astype(jnp.int32)

    def stack(at):
        start, size = chunks[at]
        return jnp.concatenate([gate_pre[:, start : start + size], up_pre[:, start : start + size]], axis=0)

    def hidden_part(at, before):
        start, size = chunks[at]
        own, *sent = partial_hidden_grad(after(here, before), grad_out_there, w_down, w_there, start, size, unit)
        return own, sent

    def send_hidden(sent):
        return [swap(block, bits) for block, bits in zip(sent, (2, 4, 6))]

    def down(at, grad_down, before):
        start, size = chunks[at]
        return grad_down_part(
            stored[at], after(grad_out_all, before), grad_down, hidden_units, 0, start, size, unit
        )

    stored = {}
    grad_out_all = lax.all_gather(grad_out, "row", axis=0, tiled=True)
    w_there = swap(w_down, 1)
    both0, both1 = stack(0), stack(1)
    x0, y0 = swap(both0, 2), swap(both0, 4)
    x0, y0 = after(x0, both1), after(y0, both1)
    over_y, over_x = x0[:part], y0[part:]
    far0 = [swap(over_y, 4), swap(over_x, 2)]
    both1 = after(both1, (over_y, over_x))
    x1, y1 = swap(both1, 2), swap(both1, 4)
    grad_out_all, for_peer = reorder(where, after(grad_out_all, (far0, w_there)))
    here = grad_out_all
    grad_out_there = swap(for_peer, 1)
    inputs_all = lax.all_gather(after(inputs, here), "row", axis=0, tiled=True)

    own0, sent0 = hidden_part(0, here)
    got0 = send_hidden(sent0)
    for_x, for_y, keep_x, keep_y = halved_hidden_grad(
        after(here, (own0, x1, y1)), grad_out_there, w_down, w_there, *chunks[1], unit
    )
    from_x, from_y = swap(for_x, 2), swap(for_y, 4)
    stored[0] = both_cores([both0, x0, y0, *[after(piece, keep_x) for piece in far0]])
    hidden0 = total_hidden_grad(after(own0, stored[0][0]), *got0)
    hidden0_all = lax.all_gather(hidden0, "col", axis=0, tiled=True)
    x1, y1 = after(x1, hidden0), after(y1, hidden0)
    over_y, over_x = x1[:part], y1[part:]
    inputs_all, _ = reorder(where, after(inputs_all, (over_y, over_x)))
    for_y, for_x, own1 = pair_sum(after(keep_x, inputs_all), from_x, keep_y, from_y)
    from_y, from_x = swap(for_y, 4), swap(for_x, 2)
    far1 = [swap(after(over_y, own1), 4), swap(after(over_x, own1), 2)]
    grad_down = down(0, None, own1)
    hidden1 = halves_sum(after(own1, grad_down), from_y, from_x)
    hidden1_all = lax.all_gather(hidden1, "col", axis=0, tiled=True)
    grad_gate, grad_up, total = first_part(
        where, hidden0_all, stored[0], after(inputs_all, hidden1), w_gate, w_up, cut, unit
    )
    stored[1] = both_cores([after(piece, total) for piece in (both1, x1, y1, *far1)])
    gate_grad, up_grad, *sums = input_part(
        where, rows, hidden1_all, stored[1], w_gate, w_up, total, *chunks[1], unit
    )
    sums = [sums[0]] + [onward(block, rows, ahead) for ahead, block in enumerate(sums) if ahead]
    earlier = (grad_gate, grad_up, grad_down)
    grad_gate, grad_up, grad_down = weight_part(
        gate_grad, up_grad, stored[1], inputs_all, grad_out_all, earlier, cut, unit // 2
    )
    grad_inputs = sum_rows([after(sums[0], grad_up)] + sums[1:])
    return grad_inputs, grad_gate, grad_up, grad_down


def on_any(inputs, grad_out, gate_pre, up_pre, w_gate, w_up, w_down):
    inputs_all = lax.all_gather(inputs, "row", axis=0, tiled=True)
    grad_out_all = lax.all_gather(grad_out, "row", axis=0, tiled=True)
    gate_all = lax.all_gather(gate_pre, "col", axis=0, tiled=True)
    up_all = lax.all_gather(up_pre, "col", axis=0, tiled=True)
    hidden_grad = lax.psum_scatter(dot(grad_out_all, w_down, 1, 1), "col", scatter_dimension=0, tiled=True)
    gate_grad, up_grad = swiglu_back(gate_pre, up_pre, hidden_grad)
    gate_grad = lax.all_gather(gate_grad, "col", axis=0, tiled=True)
    up_grad = lax.all_gather(up_grad, "col", axis=0, tiled=True)
    grad_down = dot(hidden_of(gate_all, up_all), grad_out_all, 0, 0).astype(BF16)
    grad_gate = dot(inputs_all, gate_grad, 0, 0).astype(BF16)
    grad_up = dot(inputs_all, up_grad, 0, 0).astype(BF16)
    total = dot(gate_grad, w_gate, 1, 1) + dot(up_grad, w_up, 1, 1)
    grad_inputs = lax.psum_scatter(total, "row", scatter_dimension=0, tiled=True).astype(BF16)
    return grad_inputs, grad_gate, grad_up, grad_down


def solution(mesh):
    rows, cols = mesh.shape["row"], mesh.shape["col"]
    plan = functools.partial(on_square, rows) if (rows, cols) == (4, 8) else on_any
    placed = (
        P("row", "col"),
        P("row", "col"),
        P("col", "row"),
        P("col", "row"),
        P("col", "row"),
        P("col", "row"),
        P("row", "col"),
    )
    return jax.shard_map(
        plan,
        mesh=mesh,
        in_specs=placed,
        out_specs=(P("row", "col"), P("col", "row"), P("col", "row"), P("row", "col")),
        check_vma=False,
    )
```
